768 devices in a mesh: grp: 16 (over z_hi, x), tp: 48 (over y, z_lo, core).
Axes of the slice: x: 4, y: 8, z: 12 (z_hi: 4, z_lo: 3; z = z_hi * 3 + z_lo), core: 2. Of those that a mesh axis runs over, the one named last changes fastest.
Arguments:
- tokens: bfloat16 [3072, 4096], P('grp'), may hold values from -6 to 6
- gate_weight: bfloat16 [4096, 18432], P(None, 'tp'), may hold values from -0.09375 to 0.09375
- up_weight: bfloat16 [4096, 18432], P(None, 'tp'), may hold values from -0.09375 to 0.09375
- down_weight: bfloat16 [18432, 4096], P('tp'), may hold values from -0.0625 to 0.0625
- active: int32 [3072, 18432], P('grp', 'tp'), may hold values 0 or 1
- kv_blocks: bfloat16 [256, 96, 2048], P('grp', 'tp'), may hold values from -6 to 6
- lengths: int32 [256], P('grp'), may hold values from 1 to 96
- dest: int32 [16, 16], replicated, may hold values from 0 to 15, each once within a row
Outputs:
- ffn_out: bfloat16 [3072, 4096], P('grp')
- cache: bfloat16 [256, 96, 2048], P('grp', 'tp')
The draws below stay inside these ranges and needn't reach their ends.
Inputs may be any that keep to these rules, and one draw needn't show every extreme that they name: Each row of dest names every decode group exactly once.
All inputs are finite; a program needn't handle non-finite values. No bound on the sum of `active` on one device may be relied on, other than what follows from the above.
Results may differ from the reference program's by a relative error of at most 0.005.
Values may be sent and summed in bfloat16 or wider, within the bound.
No kernel may reach another device: no remote copies, remote signals or barrier semaphores. Data moves between devices by JAX's collectives and lax.ppermute only.
A program may use at most 64 MiB of HBM per device.

```python
import jax
import jax.numpy as jnp

D = 4096
FF = 18432
TOKENS = 3072
KVW = 2048
REQS = 256
MAXLEN = 96
N_GRP = 16


def place_ends(values, stream_key, least, top_value):
    place = [jax.random.randint(jax.random.fold_in(stream_key, axis), (), 0, length) for axis, length in enumerate(values.shape)]
    longest = values.shape.index(max(values.shape))
    beside = place[:longest] + [(place[longest] + 1) % values.shape[longest]] + place[longest + 1:]
    return values.at[tuple(place)].set(least).at[tuple(beside)].set(top_value)


def block_levels(rng, dims, pieces, least, high):
    loudness, own = 1.0, jax.random.fold_in(rng, 6)
    for dim, parts in pieces:
        steps = jnp.exp(jax.random.uniform(jax.random.fold_in(own, dim), (parts,), jnp.float32, least / len(pieces), high / len(pieces)))
        loudness = loudness * jnp.repeat(steps, dims[dim] // parts).reshape([-1 if axis == dim else 1 for axis in range(len(dims))])
    return loudness


def bell_draw(own_key, extent, scale, most, split=(), kind=jnp.bfloat16):
    entries = jax.random.normal(own_key, extent, jnp.float32) * scale
    if len(split) > 0:
        entries = block_levels(own_key, extent, split, -0.22, 0.18) * entries
    return jnp.clip(entries, min=-most, max=most).astype(kind)


def setup_inputs(seed: int = 0) -> dict:
    arg_keys = jax.random.split(jax.random.key(seed), 9)
    tokens = bell_draw(arg_keys[0], (TOKENS, D), 1.0, 6.0, ((0, 16),))
    gate_weight = bell_draw(arg_keys[1], (D, FF), D ** -0.5, 0.09375, ((1, 48),))
    up_weight = bell_draw(arg_keys[2], (D, FF), D ** -0.5, 0.09375, ((1, 48),))
    down_weight = bell_draw(arg_keys[3], (FF, D), (FF // 2) ** -0.5, 0.0625, ((0, 48),))
    active = place_ends((jax.random.randint(arg_keys[4], (TOKENS, FF), 0, 2) < 1).astype(jnp.int32), jax.random.fold_in(arg_keys[4], 1), 0, 1)
    kv_blocks = bell_draw(arg_keys[5], (REQS, MAXLEN, KVW), 1.0, 6.0, ((0, 16), (1, 48)))
    lengths = place_ends(jax.random.randint(arg_keys[6], (REQS,), 1, MAXLEN + 1), jax.random.fold_in(arg_keys[6], 1), 1, MAXLEN).astype(jnp.int32)
    dest = jax.vmap(lambda own: jax.random.permutation(own, N_GRP))(jax.random.split(arg_keys[7], N_GRP)).reshape((N_GRP, N_GRP)).astype(jnp.int32)
    return dict(tokens=tokens, gate_weight=gate_weight, up_weight=up_weight, down_weight=down_weight, active=active, kv_blocks=kv_blocks, lengths=lengths, dest=dest)


def reference(tokens, gate_weight, up_weight, down_weight, active, kv_blocks, lengths, dest):
    gate = jnp.dot(tokens, gate_weight, preferred_element_type=jnp.float32)
    up = jnp.dot(tokens, up_weight, preferred_element_type=jnp.float32)
    hidden = (jax.nn.silu(gate) * up * active.astype(jnp.float32)).astype(jnp.bfloat16)
    ffn_out = jnp.dot(hidden, down_weight, preferred_element_type=jnp.float32).astype(jnp.bfloat16)
    position = jnp.arange(MAXLEN, dtype=jnp.int32)
    keep = position[None, :] < lengths[:, None]
    masked = jnp.where(keep[:, :, None], kv_blocks, jnp.zeros_like(kv_blocks))
    blocks = masked.reshape(N_GRP, N_GRP, MAXLEN, KVW)
    order = jnp.argsort(dest, axis=1).astype(jnp.int32)
    picked = jnp.take_along_axis(blocks, order[:, :, None, None], axis=1)
    cache = jnp.transpose(picked, (1, 0, 2, 3))
    return ffn_out, cache.reshape(REQS, MAXLEN, KVW).astype(jnp.bfloat16)
```

```python
import jax
import jax.numpy as jnp
from jax import lax
from jax.sharding import Mesh, PartitionSpec as P

GRP = ("zh", "x")
TP = ("y", "zl", "core")
RING = ("y", "zl")
SWAP = [(0, 1), (1, 0)]


def shards(tokens, gate_weight, up_weight, down_weight, active, kv_blocks, lengths, dest):
    bf16, f32 = jnp.bfloat16, jnp.float32
    core = lax.axis_index("core")

    pos_dev = kv_blocks.shape[1]
    position = lax.axis_index(TP) * pos_dev + lax.iota(jnp.int32, pos_dev)
    keep = position[None, :] < lengths[:, None]
    masked = jnp.where(keep[:, :, None], kv_blocks, jnp.zeros_like(kv_blocks))
    mine = lax.axis_index(GRP)
    own_row = lax.dynamic_slice_in_dim(dest, mine, 1, 0)[0]
    order = jnp.argsort(own_row)
    send_buffer = jnp.take(masked, order, axis=0)
    cache = lax.all_to_all(send_buffer, GRP, split_axis=0, concat_axis=0, tiled=True)

    gate = jnp.dot(tokens, gate_weight, preferred_element_type=f32)
    up = jnp.dot(tokens, up_weight, preferred_element_type=f32)
    hidden = (jax.nn.silu(gate) * up * active.astype(f32)).astype(bf16)

    rows, width = tokens.shape[0], down_weight.shape[1] // 2
    theirs = lax.dynamic_slice_in_dim(down_weight, (1 - core) * width, width, 1)
    ours = lax.dynamic_slice_in_dim(down_weight, core * width, width, 1)
    away = jnp.dot(hidden, theirs, preferred_element_type=f32).astype(bf16)
    arrived = lax.ppermute(away, "core", SWAP)
    total = jnp.dot(hidden, ours, preferred_element_type=f32) + arrived.astype(f32)

    chips = 24
    parts = total.astype(bf16).reshape(chips, rows // chips, width)
    parts = lax.all_to_all(parts, RING, split_axis=0, concat_axis=0, tiled=True)
    summed = jnp.sum(parts.astype(f32), axis=0).astype(bf16)

    spread = jnp.broadcast_to(summed[None], (chips, *summed.shape))
    half = lax.all_to_all(spread, RING, split_axis=0, concat_axis=0, tiled=True)
    half = half.reshape(rows, width)
    other = lax.ppermute(half, "core", SWAP)
    low = jnp.where(core == 0, half, other)
    high = jnp.where(core == 0, other, half)
    return (jnp.concatenate([low, high], axis=1), cache)


def solution(mesh):
    fine = Mesh(mesh.devices.reshape(4, 4, 8, 3, 2), GRP + TP)
    return jax.shard_map(
        shards,
        mesh=fine,
        in_specs=(
            P(GRP, None),
            P(None, TP),
            P(None, TP),
            P(TP, None),
            P(GRP, TP),
            P(GRP, TP, None),
            P(GRP),
            P(),
        ),
        out_specs=(P(GRP, None), P(GRP, TP, None)),
        check_vma=False,
    )
```

```python
import jax
import jax.numpy as jnp
from jax import lax
from jax.experimental import pallas as pl
from jax.experimental.pallas import tpu as pltpu
from jax.sharding import Mesh, PartitionSpec as P

GRP = ("zh", "x")
TP = ("y", "zl", "core")
RING = ("y", "zl")
SWAP = [(0, 1), (1, 0)]
SIDE = 4
CHIPS = 24

bf16, f32 = jnp.bfloat16, jnp.float32
MARK = jax.ShapeDtypeStruct((8, 128), f32)
VMEM = pl.BlockSpec(memory_space=pltpu.VMEM)
SMEM = pl.BlockSpec(memory_space=pltpu.SMEM)
LATER = pl.BlockSpec(memory_space=pl.ANY)


def call(body, out_shape, in_specs, out_specs, cost, **more):
    return pl.pallas_call(
        body,
        out_shape=out_shape,
        in_specs=in_specs,
        out_specs=out_specs,
        cost_estimate=pl.CostEstimate(flops=cost, bytes_accessed=cost, transcendentals=0),
        compiler_params=pltpu.CompilerParams(vmem_limit_bytes=16 * 2**20),
        **more,
    )


def sort_body(place_ref, dest_ref, lengths_ref, kv_ref, after_ref, *out_refs):
    x, mine, first = place_ref[0], place_ref[1], place_ref[2]
    row = lax.broadcasted_iota(jnp.int32, kv_ref.shape[1:], 0) + first
    for r in range(kv_ref.shape[0]):
        d = dest_ref[mine, r]
        value = kv_ref[r]
        value = jnp.where(row < lengths_ref[r], value, jnp.zeros_like(value))
        step = lax.rem(lax.rem(d, SIDE) - x + SIDE, SIDE)
        for k in range(SIDE):

            @pl.when(step == k)
            def _():
                out_refs[k][lax.div(d, SIDE)] = value


def turn_body(place_ref, *refs):
    x, zh = place_ref[0], place_ref[3]
    in_refs, out_refs = refs[:SIDE], refs[-SIDE:]
    for k in range(SIDE):
        source = lax.rem(x - k + SIDE, SIDE)
        for j in range(SIDE):
            out_refs[j][source] = in_refs[k][lax.rem(zh + j, SIDE)]


def lay_body(place_ref, *refs):
    zh = place_ref[3]
    in_refs, out_ref, mark_ref = refs[:SIDE], refs[-2], refs[-1]
    mark_ref[...] = jnp.zeros_like(mark_ref)
    for j in range(SIDE):
        source = lax.rem(zh - j + SIDE, SIDE)
        for k in range(SIDE):
            out_ref[source * SIDE + k] = in_refs[j][k]


def add_body(own_ref, arrived_ref, out_ref, mark_ref):
    mark_ref[...] = jnp.zeros_like(mark_ref)
    out_ref[...] = (own_ref[...] + arrived_ref[...].astype(f32)).astype(bf16)


def sum_body(*refs):
    parts_ref, out_ref, mark_ref = refs[0], refs[-2], refs[-1]
    mark_ref[...] = jnp.zeros_like(mark_ref)
    total = parts_ref[0].astype(f32)
    for i in range(1, CHIPS):
        total += parts_ref[i].astype(f32)
    total = total.astype(bf16)
    for i in range(CHIPS):
        out_ref[i] = total


def join_body(core_ref, half_ref, other_ref, out_ref):
    width = half_ref.shape[1]
    for core in range(2):

        @pl.when(core_ref[0] == core)
        def _():
            out_ref[:, core * width : (core + 1) * width] = half_ref[...]
            out_ref[:, (1 - core) * width : (2 - core) * width] = other_ref[...]


def after(value, mark):
    return pl.pallas_call(
        lambda value_ref, mark_ref, out_ref: None,
        out_shape=jax.ShapeDtypeStruct(value.shape, value.dtype),
        in_specs=[LATER] * 2,
        out_specs=LATER,
        input_output_aliases={0: 0},
    )(value, mark)


def shift(value, axis, k):
    if k == 0:
        return value
    return lax.ppermute(value, axis, [(i, (i + k) % SIDE) for i in range(SIDE)])


def shards(tokens, gate_weight, up_weight, down_weight, active, kv_blocks, lengths, dest):
    core = lax.axis_index("core")
    x, zh = lax.axis_index("x"), lax.axis_index("zh")
    place = jnp.stack([x, lax.axis_index(GRP), lax.axis_index(TP) * kv_blocks.shape[1], zh])

    gate = jnp.dot(tokens, gate_weight, preferred_element_type=f32)
    up = jnp.dot(tokens, up_weight, preferred_element_type=f32)
    hidden = (jax.nn.silu(gate) * up * active.astype(f32)).astype(bf16)

    rows, width = tokens.shape[0], down_weight.shape[1] // 2
    theirs = lax.dynamic_slice_in_dim(down_weight, (1 - core) * width, width, 1)
    ours = lax.dynamic_slice_in_dim(down_weight, core * width, width, 1)
    away = jnp.dot(hidden, theirs, preferred_element_type=f32).astype(bf16)
    arrived = lax.ppermute(away, "core", SWAP)
    own = jnp.dot(hidden, ours, preferred_element_type=f32)
    total, mark = call(
        add_body, [jax.ShapeDtypeStruct((rows, width), bf16), MARK], [VMEM] * 2, [VMEM] * 2, 10**6
    )(own, arrived)

    parts = total.reshape(CHIPS, rows // CHIPS, width)
    parts = lax.all_to_all(parts, RING, split_axis=0, concat_axis=0, tiled=True)

    slots = jax.ShapeDtypeStruct((SIDE, *kv_blocks.shape[1:]), bf16)
    bundles = call(sort_body, [slots] * SIDE, [SMEM, SMEM, SMEM, VMEM, LATER], [VMEM] * SIDE, 10**6)(
        place, dest, lengths, kv_blocks, mark
    )
    bundles = [shift(b, "x", k) for k, b in enumerate(bundles)]

    spread, mark = call(
        sum_body, [jax.ShapeDtypeStruct(parts.shape, bf16), MARK], [VMEM] + [LATER] * SIDE, [VMEM] * 2, 10**6
    )(parts, *bundles)

    half = lax.all_to_all(spread, RING, split_axis=0, concat_axis=0, tiled=True).reshape(rows, width)

    bundles = call(turn_body, [slots] * SIDE, [SMEM] + [VMEM] * SIDE + [LATER], [VMEM] * SIDE, 10**6)(
        place, *bundles, mark
    )
    bundles = [shift(b, "zh", k) for k, b in enumerate(bundles)]
    cache, mark = call(
        lay_body,
        [jax.ShapeDtypeStruct(kv_blocks.shape, bf16), MARK],
        [SMEM] + [VMEM] * SIDE,
        [VMEM] * 2,
        10**6,
    )(place, *bundles)

    half = after(half, mark)
    other = lax.ppermute(half, "core", SWAP)
    ffn_out = call(
        join_body, jax.ShapeDtypeStruct((rows, 2 * width), bf16), [SMEM, VMEM, VMEM], VMEM, 10**6
    )(core[None], half, other)
    return (ffn_out, cache)


def solution(mesh):
    fine = Mesh(mesh.devices.reshape(4, 4, 8, 3, 2), GRP + TP)
    return jax.shard_map(
        shards,
        mesh=fine,
        in_specs=(
            P(GRP, None),
            P(None, TP),
            P(None, TP),
            P(TP, None),
            P(GRP, TP),
            P(GRP, TP, None),
            P(GRP),
            P(),
        ),
        out_specs=(P(GRP, None), P(GRP, TP, None)),
        check_vma=False,
    )
```

```python
import jax
import jax.numpy as jnp
from jax import lax
from jax.experimental import pallas as pl
from jax.experimental.pallas import tpu as pltpu
from jax.sharding import Mesh, PartitionSpec as P

GRP = ("zh", "x")
TP = ("y", "zl", "core")
RING = ("y", "zl")
SWAP = [(0, 1), (1, 0)]
SIDE = 4
CHIPS = 24
STEPS = 4

bf16, f32 = jnp.bfloat16, jnp.float32
MARK = jax.ShapeDtypeStruct((8, 128), f32)
VMEM = pl.BlockSpec(memory_space=pltpu.VMEM)
SMEM = pl.BlockSpec(memory_space=pltpu.SMEM)
ANY = pl.BlockSpec(memory_space=pl.ANY)


def call(body, out_shape, in_specs, out_specs, **more):
    return pl.pallas_call(
        body,
        out_shape=out_shape,
        in_specs=in_specs,
        out_specs=out_specs,
        cost_estimate=pl.CostEstimate(flops=10**6, bytes_accessed=10**6, transcendentals=0),
        compiler_params=pltpu.CompilerParams(vmem_limit_bytes=16 * 2**20),
        **more,
    )


def slots_by_x0(place_ref, dest_ref, lengths_ref, kv_ref, mark_ref, keep_ref, send_ref):
    mine = place_ref[4]
    row = lax.broadcasted_iota(jnp.int32, kv_ref.shape[1:], 0) + place_ref[5]
    for r in range(kv_ref.shape[0]):
        d = dest_ref[mine, r]
        value = kv_ref[r]
        value = jnp.where(row < lengths_ref[r], value, jnp.zeros_like(value))
        spot = ((d >> 1) & 1) * 4 + (d >> 2)

        @pl.when((d & 1) == place_ref[0])
        def _():
            keep_ref[spot] = value

        @pl.when((d & 1) != place_ref[0])
        def _():
            send_ref[spot] = value


def slots_by_x1(place_ref, kept_ref, arrived_ref, keep_ref, send_ref):
    for other, in_ref in enumerate((kept_ref, arrived_ref)):
        source = place_ref[0] ^ other
        for z in range(4):
            keep_ref[source * 4 + z] = in_ref[place_ref[1] * 4 + z]
            send_ref[source * 4 + z] = in_ref[(place_ref[1] ^ 1) * 4 + z]


def slots_by_z1(place_ref, kept_ref, arrived_ref, *refs):
    keep_ref, send_ref = refs[-2:]
    for other, in_ref in enumerate((kept_ref, arrived_ref)):
        source = (place_ref[1] ^ other) * 2
        for s in range(2):
            for z in range(2):
                keep_ref[(source + s) * 2 + z] = in_ref[s * 4 + place_ref[3] * 2 + z]
                send_ref[(source + s) * 2 + z] = in_ref[s * 4 + (place_ref[3] ^ 1) * 2 + z]


def slots_by_z0(place_ref, kept_ref, arrived_ref, *refs):
    keep_ref, send_ref = refs[-2:]
    for other, in_ref in enumerate((kept_ref, arrived_ref)):
        source = (place_ref[3] ^ other) * 4
        for s in range(4):
            keep_ref[source + s] = in_ref[s * 2 + place_ref[2]]
            send_ref[source + s] = in_ref[s * 2 + (place_ref[2] ^ 1)]


def slots_in_place(place_ref, kept_ref, arrived_ref, out_ref, mark_ref):
    mark_ref[...] = jnp.zeros_like(mark_ref)
    for other, in_ref in enumerate((kept_ref, arrived_ref)):
        for z in range(2):
            source = (z * 2 + (place_ref[2] ^ other)) * 4
            for s in range(4):
                out_ref[source + s] = in_ref[z * 4 + s]


def add_body(own_ref, arrived_ref, out_ref, mark_ref):
    mark_ref[...] = jnp.zeros_like(mark_ref)
    rows = out_ref.shape[0]
    block = pl.ds(pl.multiple_of(pl.program_id(0) * rows, rows), rows)
    out_ref[...] = (own_ref[block] + arrived_ref[block].astype(f32)).astype(bf16)


def sum_body(parts_ref, *refs):
    out_ref, mark_ref, total_ref = refs[-3:]

    @pl.when(pl.program_id(0) == 0)
    def _():
        mark_ref[...] = jnp.zeros_like(mark_ref)
        total = parts_ref[0].astype(f32)
        for i in range(1, CHIPS):
            total += parts_ref[i].astype(f32)
        total_ref[...] = total.astype(bf16)

    for i in range(out_ref.shape[0]):
        out_ref[i] = total_ref[...]


def copy_body(where_ref, value_ref, *refs):
    refs[-1][...] = value_ref[...]


def half_of(out_shape, where, value, *into):
    rows, width = value.shape[0] // STEPS, value.shape[1]
    return pl.pallas_call(
        copy_body,
        out_shape=out_shape,
        grid_spec=pltpu.PrefetchScalarGridSpec(
            num_scalar_prefetch=1,
            grid=(STEPS,),
            in_specs=[pl.BlockSpec((rows, width), lambda i, w: (i, 0))] + [ANY] * len(into),
            out_specs=pl.BlockSpec((rows, width), lambda i, w: (i, w[0])),
        ),
        input_output_aliases={2: 0} if into else {},
        cost_estimate=pl.CostEstimate(flops=10**6, bytes_accessed=10**6, transcendentals=0),
        compiler_params=pltpu.CompilerParams(vmem_limit_bytes=16 * 2**20),
    )(where, value, *into)


def after(value, mark):
    return pl.pallas_call(
        lambda value_ref, mark_ref, out_ref: None,
        out_shape=jax.ShapeDtypeStruct(value.shape, value.dtype),
        in_specs=[ANY, VMEM],
        out_specs=ANY,
        input_output_aliases={0: 0},
    )(value, mark)


def flip(value, axis, bit):
    return lax.ppermute(value, axis, [(i, i ^ bit) for i in range(SIDE)])


def shards(tokens, gate_weight, up_weight, down_weight, active, kv_blocks, lengths, dest):
    core = lax.axis_index("core")
    x, zh = lax.axis_index("x"), lax.axis_index("zh")
    place = jnp.stack(
        [x & 1, x >> 1, zh & 1, zh >> 1, lax.axis_index(GRP), lax.axis_index(TP) * kv_blocks.shape[1]]
    )

    gate = jnp.dot(tokens, gate_weight, preferred_element_type=f32)
    up = jnp.dot(tokens, up_weight, preferred_element_type=f32)
    hidden = (jax.nn.silu(gate) * up * active.astype(f32)).astype(bf16)

    rows, width = tokens.shape[0], down_weight.shape[1] // 2
    theirs = lax.dynamic_slice_in_dim(down_weight, (1 - core) * width, width, 1)
    ours = lax.dynamic_slice_in_dim(down_weight, core * width, width, 1)
    away = jnp.dot(hidden, theirs, preferred_element_type=f32).astype(bf16)
    arrived = lax.ppermute(away, "core", SWAP)
    own = jnp.dot(hidden, ours, preferred_element_type=f32)
    total, mark = call(
        add_body,
        [pltpu.HBM((rows, width), bf16), MARK],
        [VMEM] * 2,
        [pl.BlockSpec((rows // STEPS, width), lambda i: (i, 0)), VMEM],
        grid=(STEPS,),
    )(own, arrived)

    parts = total.reshape(CHIPS, rows // CHIPS, width)
    parts = lax.all_to_all(parts, RING, split_axis=0, concat_axis=0, tiled=True)

    pair = [jax.ShapeDtypeStruct((8, *kv_blocks.shape[1:]), bf16)] * 2
    kept, sent = call(slots_by_x0, pair, [SMEM] * 3 + [VMEM] * 2, [VMEM] * 2)(place, dest, lengths, kv_blocks, mark)
    kept, sent = call(slots_by_x1, pair, [SMEM] + [VMEM] * 2, [VMEM] * 2)(place, kept, flip(sent, "x", 1))
    kept, sent = call(slots_by_z1, pair, [SMEM] + [VMEM] * 2, [VMEM] * 2)(place, kept, flip(sent, "x", 2))
    moved = flip(sent, "zh", 2)

    spread, mark = call(
        sum_body,
        [pltpu.HBM(parts.shape, bf16), MARK],
        [VMEM] * 2,
        [pl.BlockSpec((CHIPS // STEPS, *parts.shape[1:]), lambda i: (i, 0, 0)), VMEM],
        grid=(STEPS,),
        scratch_shapes=[pltpu.VMEM(parts.shape[1:], bf16)],
    )(parts, moved)

    half = lax.all_to_all(spread, RING, split_axis=0, concat_axis=0, tiled=True).reshape(rows, width)

    kept, sent = call(slots_by_z0, pair, [SMEM] + [VMEM] * 3, [VMEM] * 2)(place, kept, moved, mark)
    cache, mark = call(
        slots_in_place, [jax.ShapeDtypeStruct(kv_blocks.shape, bf16), MARK], [SMEM] + [VMEM] * 2, [VMEM] * 2
    )(place, kept, flip(sent, "zh", 1))

    half = after(half, mark)
    other = lax.ppermute(half, "core", SWAP)
    ffn_out = jax.ShapeDtypeStruct((rows, 2 * width), bf16)
    ffn_out = half_of(ffn_out, 1 - core[None], other, half_of(ffn_out, core[None], half))
    return (ffn_out, cache)


def solution(mesh):
    fine = Mesh(mesh.devices.reshape(4, 4, 8, 3, 2), GRP + TP)
    return jax.shard_map(
        shards,
        mesh=fine,
        in_specs=(
            P(GRP, None),
            P(None, TP),
            P(None, TP),
            P(TP, None),
            P(GRP, TP),
            P(GRP, TP, None),
            P(GRP),
            P(),
        ),
        out_specs=(P(GRP, None), P(GRP, TP, None)),
        check_vma=False,
    )
```

```python
import jax
import jax.numpy as jnp
from jax import lax
from jax.experimental import pallas as pl
from jax.experimental.pallas import tpu as pltpu
from jax.sharding import Mesh, PartitionSpec as P

GRP = ("zh", "x")
TP = ("y", "zl", "core")
RING = ("y", "zl")
SWAP = [(0, 1), (1, 0)]
SIDE = 4
CHIPS = 24
STEPS = 4

bf16, f32 = jnp.bfloat16, jnp.float32
MARK = jax.ShapeDtypeStruct((8, 128), f32)
VMEM = pl.BlockSpec(memory_space=pltpu.VMEM)
SMEM = pl.BlockSpec(memory_space=pltpu.SMEM)
ANY = pl.BlockSpec(memory_space=pl.ANY)


def call(body, out_shape, in_specs, out_specs, **more):
    return pl.pallas_call(
        body,
        out_shape=out_shape,
        in_specs=in_specs,
        out_specs=out_specs,
        cost_estimate=pl.CostEstimate(flops=10**6, bytes_accessed=10**6, transcendentals=0),
        compiler_params=pltpu.CompilerParams(vmem_limit_bytes=16 * 2**20),
        **more,
    )


def sort_body(place_ref, dest_ref, lengths_ref, kv_ref, mark_ref, *out_refs):
    x, mine, first = place_ref[0], place_ref[1], place_ref[2]
    row = lax.broadcasted_iota(jnp.int32, kv_ref.shape[1:], 0) + first
    for r in range(kv_ref.shape[0]):
        d = dest_ref[mine, r]
        value = kv_ref[r]
        value = jnp.where(row < lengths_ref[r], value, jnp.zeros_like(value))
        step = lax.rem(lax.rem(d, SIDE) - x + SIDE, SIDE)
        for k in range(SIDE):

            @pl.when(step == k)
            def _():
                out_refs[k][lax.div(d, SIDE)] = value


def turn_body(shifts, place_ref, *refs):
    x, zh = place_ref[0], place_ref[3]
    in_refs, out_refs = refs[:SIDE], refs[-len(shifts) :]
    for k in range(SIDE):
        source = lax.rem(x - k + SIDE, SIDE)
        for out_ref, j in zip(out_refs, shifts):
            out_ref[source] = in_refs[k][lax.rem(zh + j, SIDE)]


def lay_body(place_ref, *refs):
    zh = place_ref[3]
    in_refs, out_ref, mark_ref = refs[:SIDE], refs[-2], refs[-1]
    mark_ref[...] = jnp.zeros_like(mark_ref)
    for j in range(SIDE):
        source = lax.rem(zh - j + SIDE, SIDE)
        for k in range(SIDE):
            out_ref[source * SIDE + k] = in_refs[j][k]


def add_body(own_ref, arrived_ref, out_ref, mark_ref, total_ref, sems):
    mark_ref[...] = jnp.zeros_like(mark_ref)
    rows = out_ref.shape[0] // STEPS
    copies = []
    for i in range(STEPS):
        block = pl.ds(i * rows, rows)
        total_ref[block] = (own_ref[block] + arrived_ref[block].astype(f32)).astype(bf16)
        copies.append(pltpu.make_async_copy(total_ref.at[block], out_ref.at[block], sems.at[i]))
        copies[-1].start()
    for copy in copies:
        copy.wait()


def sum_body(parts_ref, after_ref, out_ref, mark_ref, total_ref, sems):
    mark_ref[...] = jnp.zeros_like(mark_ref)
    total = parts_ref[0].astype(f32)
    for i in range(1, CHIPS):
        total += parts_ref[i].astype(f32)
    total_ref[...] = total.astype(bf16)
    copies = [pltpu.make_async_copy(total_ref, out_ref.at[i], sems.at[i]) for i in range(CHIPS)]
    for copy in copies:
        copy.start()
    for copy in copies:
        copy.wait()


def half_body(which, core_ref, value_ref, *refs):
    out_ref, sem = refs[-2:]
    width = value_ref.shape[1]
    first = pl.multiple_of((core_ref[0] ^ which) * width, width)
    copy = pltpu.make_async_copy(value_ref, out_ref.at[:, pl.ds(first, width)], sem)
    copy.start()
    copy.wait()


def half_of(out_shape, which, core, value, *into):
    return call(
        lambda *refs: half_body(which, *refs),
        out_shape,
        [SMEM] + [ANY] * (1 + len(into)),
        ANY,
        scratch_shapes=[pltpu.SemaphoreType.DMA(())],
        input_output_aliases={2: 0} if into else {},
    )(core, value, *into)


def after(value, mark):
    return pl.pallas_call(
        lambda value_ref, mark_ref, out_ref: None,
        out_shape=jax.ShapeDtypeStruct(value.shape, value.dtype),
        in_specs=[ANY] * 2,
        out_specs=ANY,
        input_output_aliases={0: 0},
    )(value, mark)


def shift(value, axis, k):
    return lax.ppermute(value, axis, [(i, (i + k) % SIDE) for i in range(SIDE)])


def shards(tokens, gate_weight, up_weight, down_weight, active, kv_blocks, lengths, dest):
    core = lax.axis_index("core")
    x, zh = lax.axis_index("x"), lax.axis_index("zh")
    place = jnp.stack([x, lax.axis_index(GRP), lax.axis_index(TP) * kv_blocks.shape[1], zh])

    gate = jnp.dot(tokens, gate_weight, preferred_element_type=f32)
    up = jnp.dot(tokens, up_weight, preferred_element_type=f32)
    hidden = (jax.nn.silu(gate) * up * active.astype(f32)).astype(bf16)

    rows, width = tokens.shape[0], down_weight.shape[1] // 2
    theirs = lax.dynamic_slice_in_dim(down_weight, (1 - core) * width, width, 1)
    ours = lax.dynamic_slice_in_dim(down_weight, core * width, width, 1)
    away = jnp.dot(hidden, theirs, preferred_element_type=f32).astype(bf16)
    arrived = lax.ppermute(away, "core", SWAP)
    own = jnp.dot(hidden, ours, preferred_element_type=f32)
    total, mark = call(
        add_body,
        [pltpu.HBM((rows, width), bf16), MARK],
        [VMEM] * 2,
        [ANY, VMEM],
        scratch_shapes=[pltpu.VMEM((rows, width), bf16), pltpu.SemaphoreType.DMA((STEPS,))],
    )(own, arrived)

    parts = total.reshape(CHIPS, rows // CHIPS, width)
    parts = lax.all_to_all(parts, RING, split_axis=0, concat_axis=0, tiled=True)

    slots = jax.ShapeDtypeStruct((SIDE, *kv_blocks.shape[1:]), bf16)
    bundles = call(sort_body, [slots] * SIDE, [SMEM] * 3 + [VMEM] * 2, [VMEM] * SIDE)(
        place, dest, lengths, kv_blocks, mark
    )
    bundles = [bundles[0]] + [shift(bundles[k], "x", k) for k in range(1, SIDE)]
    first = call(lambda *refs: turn_body((0, 1), *refs), [slots] * 2, [SMEM] + [VMEM] * SIDE, [VMEM] * 2)(
        place, *bundles
    )
    moved = shift(first[1], "zh", 1)

    spread, mark = call(
        sum_body,
        [pltpu.HBM(parts.shape, bf16), MARK],
        [VMEM, ANY],
        [ANY, VMEM],
        scratch_shapes=[pltpu.VMEM(parts.shape[1:], bf16), pltpu.SemaphoreType.DMA((CHIPS,))],
    )(parts, moved)

    half = lax.all_to_all(spread, RING, split_axis=0, concat_axis=0, tiled=True).reshape(rows, width)

    others = call(lambda *refs: turn_body((2, 3), *refs), [slots] * 2, [SMEM] + [VMEM] * (SIDE + 1), [VMEM] * 2)(
        place, *bundles, mark
    )
    cache, mark = call(
        lay_body, [jax.ShapeDtypeStruct(kv_blocks.shape, bf16), MARK], [SMEM] + [VMEM] * SIDE, [VMEM] * 2
    )(place, first[0], moved, shift(others[0], "zh", 2), shift(others[1], "zh", 3))

    half = after(half, mark)
    other = lax.ppermute(half, "core", SWAP)
    ffn_out = jax.ShapeDtypeStruct((rows, 2 * width), bf16)
    ffn_out = half_of(ffn_out, 1, core[None], other, half_of(ffn_out, 0, core[None], half))
    return (ffn_out, cache)


def solution(mesh):
    fine = Mesh(mesh.devices.reshape(4, 4, 8, 3, 2), GRP + TP)
    return jax.shard_map(
        shards,
        mesh=fine,
        in_specs=(
            P(GRP, None),
            P(None, TP),
            P(None, TP),
            P(TP, None),
            P(GRP, TP),
            P(GRP, TP, None),
            P(GRP),
            P(),
        ),
        out_specs=(P(GRP, None), P(GRP, TP, None)),
        check_vma=False,
    )
```

```python
import jax
import jax.numpy as jnp
from jax import lax
from jax.experimental import pallas as pl
from jax.experimental.pallas import tpu as pltpu
from jax.sharding import Mesh, PartitionSpec as P

GRP = ("zh", "x")
TP = ("y", "zl", "core")
SWAP = [(0, 1), (1, 0)]
SIDE = 4
RING = 8
RUN = 3

bf16, f32 = jnp.bfloat16, jnp.float32
MARK = jax.ShapeDtypeStruct((8, 128), f32)
VMEM = pl.BlockSpec(memory_space=pltpu.VMEM)
SMEM = pl.BlockSpec(memory_space=pltpu.SMEM)
ANY = pl.BlockSpec(memory_space=pl.ANY)


def call(body, out_shape, in_specs, out_specs, **more):
    return pl.pallas_call(
        body,
        out_shape=out_shape,
        in_specs=in_specs,
        out_specs=out_specs,
        cost_estimate=pl.CostEstimate(flops=10**6, bytes_accessed=10**6, transcendentals=0),
        compiler_params=pltpu.CompilerParams(vmem_limit_bytes=16 * 2**20),
        **more,
    )


def sort_body(place_ref, dest_ref, lengths_ref, kv_ref, mark_ref, *out_refs):
    x, mine, first = place_ref[0], place_ref[1], place_ref[2]
    row = lax.broadcasted_iota(jnp.int32, kv_ref.shape[1:], 0) + first
    for r in range(kv_ref.shape[0]):
        d = dest_ref[mine, r]
        value = kv_ref[r]
        value = jnp.where(row < lengths_ref[r], value, jnp.zeros_like(value))
        step = lax.rem(lax.rem(d, SIDE) - x + SIDE, SIDE)
        for k in range(SIDE):

            @pl.when(step == k)
            def _():
                out_refs[k][lax.div(d, SIDE)] = value


def turn_body(shifts, place_ref, *refs):
    x, zh = place_ref[0], place_ref[3]
    in_refs, out_refs = refs[:SIDE], refs[-len(shifts) :]
    for k in range(SIDE):
        source = lax.rem(x - k + SIDE, SIDE)
        for out_ref, j in zip(out_refs, shifts):
            out_ref[source] = in_refs[k][lax.rem(zh + j, SIDE)]


def lay_body(place_ref, *refs):
    zh = place_ref[3]
    in_refs, out_ref, mark_ref = refs[:SIDE], refs[-2], refs[-1]
    mark_ref[...] = jnp.zeros_like(mark_ref)
    for j in range(SIDE):
        source = lax.rem(zh - j + SIDE, SIDE)
        for k in range(SIDE):
            out_ref[source * SIDE + k] = in_refs[j][k]


def add_body(zl_ref, own_ref, arrived_ref, keep_ref, *refs):
    rows = keep_ref.shape[0]
    refs[-1][...] = jnp.zeros_like(refs[-1])
    for k in range(RUN):
        block = pl.ds(pl.multiple_of(lax.rem(zl_ref[0] + k, RUN) * rows, rows), rows)
        total = own_ref[block] + arrived_ref[block].astype(f32)
        if k == 0:
            keep_ref[...] = total
        else:
            refs[k - 1][...] = total.astype(bf16)


def run_body(keep_ref, first_ref, second_ref, *refs):
    out_ref, mark_ref = refs[-2:]
    mark_ref[...] = jnp.zeros_like(mark_ref)
    total = keep_ref[...] + first_ref[...].astype(f32) + second_ref[...].astype(f32)
    out_ref[...] = total.astype(bf16)


def ring_body(parts_ref, after_ref, out_ref, mark_ref, total_ref, sems):
    mark_ref[...] = jnp.zeros_like(mark_ref)
    total = parts_ref[0].astype(f32)
    for i in range(1, RING):
        total += parts_ref[i].astype(f32)
    total_ref[...] = total.astype(bf16)
    copies = [pltpu.make_async_copy(total_ref, out_ref.at[i], sems.at[i]) for i in range(RING)]
    for copy in copies:
        copy.start()
    for copy in copies:
        copy.wait()


def half_body(which, core_ref, value_ref, *refs):
    out_ref, sem = refs[-2:]
    width = value_ref.shape[1]
    first = pl.multiple_of((core_ref[0] ^ which) * width, width)
    copy = pltpu.make_async_copy(value_ref, out_ref.at[:, pl.ds(first, width)], sem)
    copy.start()
    copy.wait()


def half_of(out_shape, which, core, value, *into):
    return call(
        lambda *refs: half_body(which, *refs),
        out_shape,
        [SMEM, VMEM] + [ANY] * len(into),
        ANY,
        scratch_shapes=[pltpu.SemaphoreType.DMA(())],
        input_output_aliases={2: 0} if into else {},
    )(core, value, *into)


def after(value, mark):
    return pl.pallas_call(
        lambda value_ref, mark_ref, out_ref: None,
        out_shape=jax.ShapeDtypeStruct(value.shape, value.dtype),
        in_specs=[ANY] * 2,
        out_specs=ANY,
        input_output_aliases={0: 0},
    )(value, mark)


def shift(value, axis, k, size=SIDE):
    return lax.ppermute(value, axis, [(i, (i + k) % size) for i in range(size)])


def shards(tokens, gate_weight, up_weight, down_weight, active, kv_blocks, lengths, dest):
    core = lax.axis_index("core")
    x, zh = lax.axis_index("x"), lax.axis_index("zh")
    place = jnp.stack([x, lax.axis_index(GRP), lax.axis_index(TP) * kv_blocks.shape[1], zh])

    gate = jnp.dot(tokens, gate_weight, preferred_element_type=f32)
    up = jnp.dot(tokens, up_weight, preferred_element_type=f32)
    hidden = (jax.nn.silu(gate) * up * active.astype(f32)).astype(bf16)

    rows, width = tokens.shape[0], down_weight.shape[1] // 2
    theirs = lax.dynamic_slice_in_dim(down_weight, (1 - core) * width, width, 1)
    ours = lax.dynamic_slice_in_dim(down_weight, core * width, width, 1)
    away = jnp.dot(hidden, theirs, preferred_element_type=f32).astype(bf16)
    arrived = lax.ppermute(away, "core", SWAP)
    own = jnp.dot(hidden, ours, preferred_element_type=f32)
    piece = rows // RUN
    keep, *sends, mark = call(
        add_body,
        [pltpu.HBM((piece, width), f32)] + [jax.ShapeDtypeStruct((piece, width), bf16)] * 2 + [MARK],
        [SMEM] + [VMEM] * 2,
        [VMEM] * 4,
    )(lax.axis_index("zl")[None], own, arrived)

    sends = [shift(sends[k - 1], "zl", k, RUN) for k in range(1, RUN)]

    slots = jax.ShapeDtypeStruct((SIDE, *kv_blocks.shape[1:]), bf16)
    bundles = call(sort_body, [slots] * SIDE, [SMEM] * 3 + [VMEM] * 2, [VMEM] * SIDE)(
        place, dest, lengths, kv_blocks, mark
    )
    bundles = [bundles[0]] + [shift(bundles[k], "x", k) for k in range(1, SIDE)]

    total, mark = call(
        run_body, [pltpu.HBM((piece, width), bf16), MARK], [VMEM] * 3 + [ANY] * 3, [VMEM] * 2
    )(keep, *sends, *bundles[1:])
    parts = total.reshape(RING, piece // RING, width)
    parts = lax.all_to_all(parts, "y", split_axis=0, concat_axis=0, tiled=True)

    first = call(lambda *refs: turn_body((0, 1), *refs), [slots] * 2, [SMEM] + [VMEM] * (SIDE + 1), [VMEM] * 2)(
        place, *bundles, mark
    )
    moved = shift(first[1], "zh", 1)

    spread, mark = call(
        ring_body,
        [pltpu.HBM(parts.shape, bf16), MARK],
        [VMEM, ANY],
        [ANY, VMEM],
        scratch_shapes=[pltpu.VMEM(parts.shape[1:], bf16), pltpu.SemaphoreType.DMA((RING,))],
    )(parts, moved)

    third = lax.all_to_all(spread, "y", split_axis=0, concat_axis=0, tiled=True).reshape(piece, width)

    others = call(lambda *refs: turn_body((2, 3), *refs), [slots] * 2, [SMEM] + [VMEM] * (SIDE + 1), [VMEM] * 2)(
        place, *bundles, mark
    )
    cache, mark = call(
        lay_body, [jax.ShapeDtypeStruct(kv_blocks.shape, bf16), MARK], [SMEM] + [VMEM] * SIDE, [VMEM] * 2
    )(place, first[0], moved, shift(others[0], "zh", 2), shift(others[1], "zh", 3))

    half = lax.all_gather(after(third, mark), "zl", axis=0, tiled=True)
    other = lax.ppermute(half, "core", SWAP)
    ffn_out = jax.ShapeDtypeStruct((rows, 2 * width), bf16)
    ffn_out = half_of(ffn_out, 1, core[None], other, half_of(ffn_out, 0, core[None], half))
    return (ffn_out, cache)


def solution(mesh):
    fine = Mesh(mesh.devices.reshape(4, 4, 8, 3, 2), GRP + TP)
    return jax.shard_map(
        shards,
        mesh=fine,
        in_specs=(
            P(GRP, None),
            P(None, TP),
            P(None, TP),
            P(TP, None),
            P(GRP, TP),
            P(GRP, TP, None),
            P(GRP),
            P(),
        ),
        out_specs=(P(GRP, None), P(GRP, TP, None)),
        check_vma=False,
    )
```

```python
import jax
import jax.numpy as jnp
from jax import lax
from jax.experimental import pallas as pl
from jax.experimental.pallas import tpu as pltpu
from jax.sharding import Mesh, PartitionSpec as P

GRP = ("zh", "x")
TP = ("y", "zl", "core")
RING = ("y", "zl")
SWAP = [(0, 1), (1, 0)]
SIDE = 4
CHIPS = 24
STEPS = 4

bf16, f32 = jnp.bfloat16, jnp.float32
MARK = jax.ShapeDtypeStruct((8, 128), f32)
VMEM = pl.BlockSpec(memory_space=pltpu.VMEM)
SMEM = pl.BlockSpec(memory_space=pltpu.SMEM)
ANY = pl.BlockSpec(memory_space=pl.ANY)


def call(body, out_shape, in_specs, out_specs, **more):
    return pl.pallas_call(
        body,
        out_shape=out_shape,
        in_specs=in_specs,
        out_specs=out_specs,
        cost_estimate=pl.CostEstimate(flops=10**6, bytes_accessed=10**6, transcendentals=0),
        compiler_params=pltpu.CompilerParams(vmem_limit_bytes=16 * 2**20),
        **more,
    )


def slots_by_z1(place_ref, dest_ref, lengths_ref, kv_ref, keep_ref, send_ref):
    mine = place_ref[4]
    row = lax.broadcasted_iota(jnp.int32, kv_ref.shape[1:], 0) + place_ref[5]
    for r in range(kv_ref.shape[0]):
        d = dest_ref[mine, r]
        value = kv_ref[r]
        value = jnp.where(row < lengths_ref[r], value, jnp.zeros_like(value))
        spot = (d & 1) * 4 + ((d >> 1) & 1) * 2 + ((d >> 2) & 1)

        @pl.when(((d >> 3) & 1) == place_ref[3])
        def _():
            keep_ref[spot] = value

        @pl.when(((d >> 3) & 1) != place_ref[3])
        def _():
            send_ref[spot] = value


def slots_by_x0(place_ref, kept_ref, arrived_ref, keep_ref, send_ref):
    for other, in_ref in enumerate((kept_ref, arrived_ref)):
        source = (place_ref[3] ^ other) * 4
        for r in range(4):
            keep_ref[source + r] = in_ref[place_ref[0] * 4 + r]
            send_ref[source + r] = in_ref[(place_ref[0] ^ 1) * 4 + r]


def slots_by_x1(place_ref, kept_ref, arrived_ref, after_ref, keep_ref, send_ref):
    for other, in_ref in enumerate((kept_ref, arrived_ref)):
        source = (place_ref[0] ^ other) * 4
        for s in range(2):
            for z in range(2):
                keep_ref[source + s * 2 + z] = in_ref[s * 4 + place_ref[1] * 2 + z]
                send_ref[source + s * 2 + z] = in_ref[s * 4 + (place_ref[1] ^ 1) * 2 + z]


def slots_by_z0(place_ref, kept_ref, arrived_ref, keep_ref, send_ref):
    for other, in_ref in enumerate((kept_ref, arrived_ref)):
        source = (place_ref[1] ^ other) * 4
        for s in range(4):
            keep_ref[source + s] = in_ref[s * 2 + place_ref[2]]
            send_ref[source + s] = in_ref[s * 2 + (place_ref[2] ^ 1)]


def slots_in_place(place_ref, kept_ref, arrived_ref, out_ref, mark_ref):
    mark_ref[...] = jnp.zeros_like(mark_ref)
    for other, in_ref in enumerate((kept_ref, arrived_ref)):
        for z in range(2):
            source = (z * 2 + (place_ref[2] ^ other)) * 4
            for s in range(4):
                out_ref[source + s] = in_ref[s * 2 + z]


def sum_body(parts_ref, after_ref, out_ref, mark_ref, held_ref, total_ref, in_sems, out_sems):
    mark_ref[...] = jnp.zeros_like(mark_ref)
    count = CHIPS // STEPS
    blocks = [pl.ds(i * count, count) for i in range(STEPS)]
    loads = [pltpu.make_async_copy(parts_ref.at[b], held_ref.at[b], in_sems.at[i]) for i, b in enumerate(blocks)]
    for load in loads:
        load.start()
    total = jnp.zeros(total_ref.shape, f32)
    for i, load in enumerate(loads):
        load.wait()
        for k in range(i * count, (i + 1) * count):
            total += held_ref[k].astype(f32)
    total_ref[...] = total.astype(bf16)
    copies = [pltpu.make_async_copy(total_ref, out_ref.at[i], out_sems.at[i]) for i in range(CHIPS)]
    for copy in copies:
        copy.start()
    for copy in copies:
        copy.wait()


def half_body(which, core_ref, value_ref, *refs):
    out_ref, sem = refs[-2:]
    width = value_ref.shape[1]
    first = pl.multiple_of((core_ref[0] ^ which) * width, width)
    copy = pltpu.make_async_copy(value_ref, out_ref.at[:, pl.ds(first, width)], sem)
    copy.start()
    copy.wait()


def half_of(out_shape, which, core, value, *into):
    return call(
        lambda *refs: half_body(which, *refs),
        out_shape,
        [SMEM, VMEM] + [ANY] * len(into),
        ANY,
        scratch_shapes=[pltpu.SemaphoreType.DMA(())],
        input_output_aliases={2: 0} if into else {},
    )(core, value, *into)


def after(value, mark):
    return pl.pallas_call(
        lambda value_ref, mark_ref, out_ref: None,
        out_shape=jax.ShapeDtypeStruct(value.shape, value.dtype),
        in_specs=[ANY] * 2,
        out_specs=ANY,
        input_output_aliases={0: 0},
    )(value, mark)


def flip(value, axis, bit):
    return lax.ppermute(value, axis, [(i, i ^ bit) for i in range(SIDE)])


def shards(tokens, gate_weight, up_weight, down_weight, active, kv_blocks, lengths, dest):
    core = lax.axis_index("core")
    x, zh = lax.axis_index("x"), lax.axis_index("zh")
    place = jnp.stack(
        [x & 1, x >> 1, zh & 1, zh >> 1, lax.axis_index(GRP), lax.axis_index(TP) * kv_blocks.shape[1]]
    )

    gate = jnp.dot(tokens, gate_weight, preferred_element_type=f32)
    up = jnp.dot(tokens, up_weight, preferred_element_type=f32)
    hidden = (jax.nn.silu(gate) * up * active.astype(f32)).astype(bf16)

    rows, width = tokens.shape[0], down_weight.shape[1] // 2
    theirs = lax.dynamic_slice_in_dim(down_weight, (1 - core) * width, width, 1)
    ours = lax.dynamic_slice_in_dim(down_weight, core * width, width, 1)
    away = jnp.dot(hidden, theirs, preferred_element_type=f32).astype(bf16)
    arrived = lax.ppermute(away, "core", SWAP)
    total = jnp.dot(hidden, ours, preferred_element_type=f32) + arrived.astype(f32)

    total = total.astype(bf16).reshape(CHIPS, rows // CHIPS, width)
    parts = lax.all_to_all(total, RING, split_axis=0, concat_axis=0, tiled=True)

    pair = [jax.ShapeDtypeStruct((8, *kv_blocks.shape[1:]), bf16)] * 2
    kept, sent = call(slots_by_z1, pair, [SMEM] * 3 + [VMEM], [VMEM] * 2)(place, dest, lengths, kv_blocks)
    kept, sent = call(slots_by_x0, pair, [SMEM] + [VMEM] * 2, [VMEM] * 2)(place, kept, flip(sent, "zh", 2))
    moved = flip(sent, "x", 1)

    spread, mark = call(
        sum_body,
        [pltpu.HBM(parts.shape, bf16), MARK],
        [ANY] * 2,
        [ANY, VMEM],
        scratch_shapes=[
            pltpu.VMEM(parts.shape, bf16),
            pltpu.VMEM(parts.shape[1:], bf16),
            pltpu.SemaphoreType.DMA((STEPS,)),
            pltpu.SemaphoreType.DMA((CHIPS,)),
        ],
    )(parts, moved)

    half = lax.all_to_all(spread, RING, split_axis=0, concat_axis=0, tiled=True).reshape(rows, width)

    kept, sent = call(slots_by_x1, pair, [SMEM] + [VMEM] * 3, [VMEM] * 2)(place, kept, moved, mark)
    kept, sent = call(slots_by_z0, pair, [SMEM] + [VMEM] * 2, [VMEM] * 2)(place, kept, flip(sent, "x", 2))
    cache, mark = call(
        slots_in_place, [jax.ShapeDtypeStruct(kv_blocks.shape, bf16), MARK], [SMEM] + [VMEM] * 2, [VMEM] * 2
    )(place, kept, flip(sent, "zh", 1))

    half = after(half, mark)
    other = lax.ppermute(half, "core", SWAP)
    ffn_out = jax.ShapeDtypeStruct((rows, 2 * width), bf16)
    ffn_out = half_of(ffn_out, 1, core[None], other, half_of(ffn_out, 0, core[None], half))
    return (ffn_out, cache)


def solution(mesh):
    fine = Mesh(mesh.devices.reshape(4, 4, 8, 3, 2), GRP + TP)
    return jax.shard_map(
        shards,
        mesh=fine,
        in_specs=(
            P(GRP, None),
            P(None, TP),
            P(None, TP),
            P(TP, None),
            P(GRP, TP),
            P(GRP, TP, None),
            P(GRP),
            P(),
        ),
        out_specs=(P(GRP, None), P(GRP, TP, None)),
        check_vma=False,
    )
```

```python
import jax
import jax.numpy as jnp
from jax import lax
from jax.experimental import pallas as pl
from jax.experimental.pallas import tpu as pltpu
from jax.sharding import Mesh, PartitionSpec as P

GRP = ("zh", "x")
TP = ("y", "zl", "core")
RING = ("y", "zl")
SWAP = [(0, 1), (1, 0)]
SIDE = 4
CHIPS = 24
STEPS = 4

bf16, f32 = jnp.bfloat16, jnp.float32
MARK = jax.ShapeDtypeStruct((8, 128), f32)
VMEM = pl.BlockSpec(memory_space=pltpu.VMEM)
SMEM = pl.BlockSpec(memory_space=pltpu.SMEM)
ANY = pl.BlockSpec(memory_space=pl.ANY)


def call(body, out_shape, in_specs, out_specs, **more):
    return pl.pallas_call(
        body,
        out_shape=out_shape,
        in_specs=in_specs,
        out_specs=out_specs,
        cost_estimate=pl.CostEstimate(flops=10**6, bytes_accessed=10**6, transcendentals=0),
        compiler_params=pltpu.CompilerParams(vmem_limit_bytes=16 * 2**20),
        **more,
    )


def sort_body(place_ref, dest_ref, lengths_ref, kv_ref, *refs):
    out_refs, mark_ref = refs[:SIDE], refs[SIDE]
    mark_ref[...] = jnp.zeros_like(mark_ref)
    x, mine, first = place_ref[0], place_ref[1], place_ref[2]
    row = lax.broadcasted_iota(jnp.int32, kv_ref.shape[1:], 0) + first
    for r in range(kv_ref.shape[0]):
        d = dest_ref[mine, r]
        value = kv_ref[r]
        value = jnp.where(row < lengths_ref[r], value, jnp.zeros_like(value))
        step = lax.rem(lax.rem(d, SIDE) - x + SIDE, SIDE)
        for k in range(SIDE):

            @pl.when(step == k)
            def _():
                out_refs[k][lax.div(d, SIDE)] = value


def turn_body(place_ref, *refs):
    x, zh = place_ref[0], place_ref[3]
    in_refs, out_refs = refs[:SIDE], refs[SIDE:]
    for k in range(SIDE):
        source = lax.rem(x - k + SIDE, SIDE)
        for j, out_ref in enumerate(out_refs):
            out_ref[source] = in_refs[k][lax.rem(zh + j, SIDE)]


def lay_body(place_ref, *refs):
    zh = place_ref[3]
    in_refs, out_ref = refs[:SIDE], refs[-1]
    for j in range(SIDE):
        source = lax.rem(zh - j + SIDE, SIDE)
        for k in range(SIDE):
            out_ref[source * SIDE + k] = in_refs[j][k]


def add_body(own_ref, arrived_ref, after_ref, out_ref, total_ref, sems):
    rows = out_ref.shape[0] // STEPS
    copies = []
    for i in range(STEPS):
        block = pl.ds(i * rows, rows)
        total_ref[block] = (own_ref[block] + arrived_ref[block].astype(f32)).astype(bf16)
        copies.append(pltpu.make_async_copy(total_ref.at[block], out_ref.at[block], sems.at[i]))
        copies[-1].start()
    for copy in copies:
        copy.wait()


def sum_body(parts_ref, *refs):
    out_ref, total_ref, sems = refs[-3:]
    total = parts_ref[0].astype(f32)
    for i in range(1, CHIPS):
        total += parts_ref[i].astype(f32)
    total_ref[...] = total.astype(bf16)
    copies = [pltpu.make_async_copy(total_ref, out_ref.at[i], sems.at[i]) for i in range(CHIPS)]
    for copy in copies:
        copy.start()
    for copy in copies:
        copy.wait()


def half_body(which, core_ref, value_ref, *refs):
    out_ref, sem = refs[-2:]
    width = value_ref.shape[1]
    first = pl.multiple_of((core_ref[0] ^ which) * width, width)
    copy = pltpu.make_async_copy(value_ref, out_ref.at[:, pl.ds(first, width)], sem)
    copy.start()
    copy.wait()


def half_of(out_shape, which, core, value, *into):
    return call(
        lambda *refs: half_body(which, *refs),
        out_shape,
        [SMEM, VMEM] + [ANY] * len(into),
        ANY,
        scratch_shapes=[pltpu.SemaphoreType.DMA(())],
        input_output_aliases={2: 0} if into else {},
    )(core, value, *into)


def after(value, *others):
    return call(
        lambda *refs: None,
        jax.ShapeDtypeStruct(value.shape, value.dtype),
        [ANY] * (1 + len(others)),
        ANY,
        input_output_aliases={0: 0},
    )(value, *others)


def shift(value, axis, k):
    return lax.ppermute(value, axis, [(i, (i + k) % SIDE) for i in range(SIDE)])


def shards(tokens, gate_weight, up_weight, down_weight, active, kv_blocks, lengths, dest):
    core = lax.axis_index("core")
    x, zh = lax.axis_index("x"), lax.axis_index("zh")
    place = jnp.stack([x, lax.axis_index(GRP), lax.axis_index(TP) * kv_blocks.shape[1], zh])

    slots = jax.ShapeDtypeStruct((SIDE, *kv_blocks.shape[1:]), bf16)
    *bundles, mark = call(sort_body, [slots] * SIDE + [MARK], [SMEM] * 3 + [VMEM], [VMEM] * (SIDE + 1))(
        place, dest, lengths, kv_blocks
    )

    gate = jnp.dot(tokens, gate_weight, preferred_element_type=f32)
    up = jnp.dot(tokens, up_weight, preferred_element_type=f32)
    hidden = (jax.nn.silu(gate) * up * active.astype(f32)).astype(bf16)

    rows, width = tokens.shape[0], down_weight.shape[1] // 2
    theirs = lax.dynamic_slice_in_dim(down_weight, (1 - core) * width, width, 1)
    ours = lax.dynamic_slice_in_dim(down_weight, core * width, width, 1)
    away = jnp.dot(hidden, theirs, preferred_element_type=f32).astype(bf16)
    arrived = lax.ppermute(away, "core", SWAP)
    own = jnp.dot(hidden, ours, preferred_element_type=f32)
    total = call(
        add_body,
        pltpu.HBM((rows, width), bf16),
        [VMEM] * 3,
        ANY,
        scratch_shapes=[pltpu.VMEM((rows, width), bf16), pltpu.SemaphoreType.DMA((STEPS,))],
    )(own, arrived, mark)

    parts = total.reshape(CHIPS, rows // CHIPS, width)
    parts = lax.all_to_all(parts, RING, split_axis=0, concat_axis=0, tiled=True)

    bundles = [bundles[0]] + [shift(bundles[k], "x", k) for k in range(1, SIDE)]
    bundles = call(turn_body, [slots] * SIDE, [SMEM] + [VMEM] * SIDE, [VMEM] * SIDE)(place, *bundles)

    spread = call(
        sum_body,
        pltpu.HBM(parts.shape, bf16),
        [VMEM] + [ANY] * SIDE,
        ANY,
        scratch_shapes=[pltpu.VMEM(parts.shape[1:], bf16), pltpu.SemaphoreType.DMA((CHIPS,))],
    )(parts, *bundles)

    half = lax.all_to_all(spread, RING, split_axis=0, concat_axis=0, tiled=True).reshape(rows, width)

    bundles = [bundles[0]] + [shift(bundles[k], "zh", k) for k in range(1, SIDE)]
    cache = call(lay_body, jax.ShapeDtypeStruct(kv_blocks.shape, bf16), [SMEM] + [VMEM] * SIDE, VMEM)(place, *bundles)

    half = after(half, *bundles[1:])
    other = lax.ppermute(half, "core", SWAP)
    ffn_out = jax.ShapeDtypeStruct((rows, 2 * width), bf16)
    ffn_out = half_of(ffn_out, 1, core[None], other, half_of(ffn_out, 0, core[None], half))
    return (ffn_out, cache)


def solution(mesh):
    fine = Mesh(mesh.devices.reshape(4, 4, 8, 3, 2), GRP + TP)
    return jax.shard_map(
        shards,
        mesh=fine,
        in_specs=(
            P(GRP, None),
            P(None, TP),
            P(None, TP),
            P(TP, None),
            P(GRP, TP),
            P(GRP, TP, None),
            P(GRP),
            P(),
        ),
        out_specs=(P(GRP, None), P(GRP, TP, None)),
        check_vma=False,
    )
```

```python
import jax
import jax.numpy as jnp
from jax import lax
from jax.experimental import pallas as pl
from jax.experimental.pallas import tpu as pltpu
from jax.sharding import Mesh, PartitionSpec as P

GRP = ("zh", "x")
TP = ("y", "zl", "core")
RING = ("y", "zl")
SWAP = [(0, 1), (1, 0)]
SIDE = 4
CHIPS = 24
ORDER = (0, 2, 1, 3)
STEPS = 4

bf16, f32 = jnp.bfloat16, jnp.float32
MARK = jax.ShapeDtypeStruct((8, 128), f32)
VMEM = pl.BlockSpec(memory_space=pltpu.VMEM)
SMEM = pl.BlockSpec(memory_space=pltpu.SMEM)
ANY = pl.BlockSpec(memory_space=pl.ANY)


def call(body, out_shape, in_specs, out_specs, **more):
    return pl.pallas_call(
        body,
        out_shape=out_shape,
        in_specs=in_specs,
        out_specs=out_specs,
        cost_estimate=pl.CostEstimate(flops=10**6, bytes_accessed=10**6, transcendentals=0),
        compiler_params=pltpu.CompilerParams(vmem_limit_bytes=16 * 2**20),
        **more,
    )


def sort_body(place_ref, dest_ref, lengths_ref, kv_ref, mark_ref, *out_refs):
    x, mine, first = place_ref[0], place_ref[1], place_ref[2]
    row = lax.broadcasted_iota(jnp.int32, kv_ref.shape[1:], 0) + first
    for r in range(kv_ref.shape[0]):
        d = dest_ref[mine, r]
        value = kv_ref[r]
        value = jnp.where(row < lengths_ref[r], value, jnp.zeros_like(value))
        step = lax.rem(lax.rem(d, SIDE) - x + SIDE, SIDE)
        for k in range(SIDE):

            @pl.when(step == k)
            def _():
                out_refs[k][lax.div(d, SIDE)] = value


def turn_body(place_ref, *refs):
    x, zh = place_ref[0], place_ref[3]
    in_refs, out_refs = refs[:SIDE], refs[SIDE:]
    for k in range(SIDE):
        source = lax.rem(x - k + SIDE, SIDE)
        for out_ref, j in zip(out_refs, ORDER):
            out_ref[source] = in_refs[k][lax.rem(zh + j, SIDE)]


def lay_body(place_ref, *refs):
    zh = place_ref[3]
    in_refs, out_ref = refs[:SIDE], refs[-1]
    for in_ref, j in zip(in_refs, ORDER):
        source = lax.rem(zh - j + SIDE, SIDE)
        for k in range(SIDE):
            out_ref[source * SIDE + k] = in_ref[k]


def add_body(own_ref, arrived_ref, out_ref, mark_ref, total_ref, sems):
    mark_ref[...] = jnp.zeros_like(mark_ref)
    rows = out_ref.shape[0] // STEPS
    copies = []
    for i in range(STEPS):
        block = pl.ds(i * rows, rows)
        total_ref[block] = (own_ref[block] + arrived_ref[block].astype(f32)).astype(bf16)
        copies.append(pltpu.make_async_copy(total_ref.at[block], out_ref.at[block], sems.at[i]))
        copies[-1].start()
    for copy in copies:
        copy.wait()


def sum_body(parts_ref, *refs):
    out_ref, total_ref, sems = refs[-3:]
    total = parts_ref[0].astype(f32)
    for i in range(1, CHIPS):
        total += parts_ref[i].astype(f32)
    total_ref[...] = total.astype(bf16)
    copies = [pltpu.make_async_copy(total_ref, out_ref.at[i], sems.at[i]) for i in range(CHIPS)]
    for copy in copies:
        copy.start()
    for copy in copies:
        copy.wait()


def half_body(which, core_ref, value_ref, *refs):
    if which == 0:
        out_ref, held_ref, in_sems, out_sems = refs
    else:
        out_ref, out_sems = refs[-2:]
        held_ref = value_ref
    rows, width = value_ref.shape[0] // STEPS, value_ref.shape[1]
    first = pl.multiple_of((core_ref[0] ^ which) * width, width)
    blocks = [pl.ds(i * rows, rows) for i in range(STEPS)]
    stores = [
        pltpu.make_async_copy(held_ref.at[b], out_ref.at[b, pl.ds(first, width)], out_sems.at[i])
        for i, b in enumerate(blocks)
    ]
    if which == 0:
        loads = [pltpu.make_async_copy(value_ref.at[b], held_ref.at[b], in_sems.at[i]) for i, b in enumerate(blocks)]
        for load in loads:
            load.start()
        for load, store in zip(loads, stores):
            load.wait()
            store.start()
    else:
        for store in stores:
            store.start()
    for store in stores:
        store.wait()


def half_of(out_shape, core, value, *into):
    sems = pltpu.SemaphoreType.DMA((STEPS,))
    return call(
        lambda *refs: half_body(len(into), *refs),
        out_shape,
        [SMEM, VMEM if into else ANY] + [ANY] * len(into),
        ANY,
        scratch_shapes=[sems] if into else [pltpu.VMEM(value.shape, bf16), sems, sems],
        input_output_aliases={2: 0} if into else {},
    )(core, value, *into)


def after(value, *others):
    return call(
        lambda *refs: None,
        jax.ShapeDtypeStruct(value.shape, value.dtype),
        [ANY] * (1 + len(others)),
        ANY,
        input_output_aliases={0: 0},
    )(value, *others)


def shift(value, axis, k):
    return lax.ppermute(value, axis, [(i, (i + k) % SIDE) for i in range(SIDE)])


def shards(tokens, gate_weight, up_weight, down_weight, active, kv_blocks, lengths, dest):
    core = lax.axis_index("core")
    x, zh = lax.axis_index("x"), lax.axis_index("zh")
    place = jnp.stack([x, lax.axis_index(GRP), lax.axis_index(TP) * kv_blocks.shape[1], zh])

    gate = jnp.dot(tokens, gate_weight, preferred_element_type=f32)
    up = jnp.dot(tokens, up_weight, preferred_element_type=f32)
    hidden = (jax.nn.silu(gate) * up * active.astype(f32)).astype(bf16)

    rows, width = tokens.shape[0], down_weight.shape[1] // 2
    theirs = lax.dynamic_slice_in_dim(down_weight, (1 - core) * width, width, 1)
    ours = lax.dynamic_slice_in_dim(down_weight, core * width, width, 1)
    away = jnp.dot(hidden, theirs, preferred_element_type=f32).astype(bf16)
    arrived = lax.ppermute(away, "core", SWAP)
    own = jnp.dot(hidden, ours, preferred_element_type=f32)
    total, mark = call(
        add_body,
        [pltpu.HBM((rows, width), bf16), MARK],
        [VMEM] * 2,
        [ANY, VMEM],
        scratch_shapes=[pltpu.VMEM((rows, width), bf16), pltpu.SemaphoreType.DMA((STEPS,))],
    )(own, arrived)

    parts = total.reshape(CHIPS, rows // CHIPS, width)
    parts = lax.all_to_all(parts, RING, split_axis=0, concat_axis=0, tiled=True)

    slots = jax.ShapeDtypeStruct((SIDE, *kv_blocks.shape[1:]), bf16)
    bundles = call(sort_body, [slots] * SIDE, [SMEM] * 3 + [VMEM] * 2, [VMEM] * SIDE)(
        place, dest, lengths, kv_blocks, mark
    )
    bundles = [bundles[0]] + [shift(bundles[k], "x", k) for k in range(1, SIDE)]
    bundles = call(turn_body, [slots] * SIDE, [SMEM] + [VMEM] * SIDE, [VMEM] * SIDE)(place, *bundles)

    spread = call(
        sum_body,
        pltpu.HBM(parts.shape, bf16),
        [VMEM] + [ANY] * SIDE,
        ANY,
        scratch_shapes=[pltpu.VMEM(parts.shape[1:], bf16), pltpu.SemaphoreType.DMA((CHIPS,))],
    )(parts, *bundles)

    half = lax.all_to_all(spread, RING, split_axis=0, concat_axis=0, tiled=True).reshape(rows, width)

    bundles = [bundles[0]] + [shift(b, "zh", j) for b, j in zip(bundles[1:], ORDER[1:])]
    cache = call(lay_body, jax.ShapeDtypeStruct(kv_blocks.shape, bf16), [SMEM] + [VMEM] * SIDE, VMEM)(place, *bundles)

    half = after(half, *bundles[1:])
    other = lax.ppermute(half, "core", SWAP)
    ffn_out = jax.ShapeDtypeStruct((rows, 2 * width), bf16)
    ffn_out = half_of(ffn_out, core[None], other, half_of(ffn_out, core[None], half))
    return (ffn_out, cache)


def solution(mesh):
    fine = Mesh(mesh.devices.reshape(4, 4, 8, 3, 2), GRP + TP)
    return jax.shard_map(
        shards,
        mesh=fine,
        in_specs=(
            P(GRP, None),
            P(None, TP),
            P(None, TP),
            P(TP, None),
            P(GRP, TP),
            P(GRP, TP, None),
            P(GRP),
            P(),
        ),
        out_specs=(P(GRP, None), P(GRP, TP, None)),
        check_vma=False,
    )
```

```python
import jax
import jax.numpy as jnp
from jax import lax
from jax.experimental import pallas as pl
from jax.experimental.pallas import tpu as pltpu
from jax.sharding import Mesh, PartitionSpec as P

GRP = ("zh", "x")
TP = ("y", "zl", "core")
RING = ("y", "zl")
SWAP = [(0, 1), (1, 0)]
SIDE = 4
CHIPS = 24
ORDER = (0, 2, 1, 3)
CHUNKS = 8
STEPS = 4

bf16, f32 = jnp.bfloat16, jnp.float32
MARK = jax.ShapeDtypeStruct((8, 128), f32)
VMEM = pl.BlockSpec(memory_space=pltpu.VMEM)
SMEM = pl.BlockSpec(memory_space=pltpu.SMEM)
ANY = pl.BlockSpec(memory_space=pl.ANY)


def call(body, out_shape, in_specs, out_specs, vmem=16, **more):
    return pl.pallas_call(
        body,
        out_shape=out_shape,
        in_specs=in_specs,
        out_specs=out_specs,
        cost_estimate=pl.CostEstimate(flops=10**6, bytes_accessed=10**6, transcendentals=0),
        compiler_params=pltpu.CompilerParams(vmem_limit_bytes=vmem * 2**20),
        **more,
    )


def hidden_body(core_ref, tokens_ref, gate_ref, up_ref, down_ref, active_ref, hidden_ref, away_ref, *scratch):
    *held, theirs_ref, mask_ref, sent_ref, sems, last_sems, out_sems = scratch
    depth = tokens_ref.shape[1] // CHUNKS
    copies = []
    for i in range(CHUNKS):
        block = pl.ds(i * depth, depth)
        pieces = zip((tokens_ref, gate_ref, up_ref), held, ((slice(None), block), (block,), (block,)))
        copies.append(
            [
                pltpu.make_async_copy(ref.at[place], to.at[place], sems.at[n, i])
                for n, (ref, to, place) in enumerate(pieces)
            ]
        )
    width = away_ref.shape[1]
    first = pl.multiple_of((1 - core_ref[0]) * width, width)
    last = [
        pltpu.make_async_copy(active_ref, mask_ref, last_sems.at[0]),
        pltpu.make_async_copy(down_ref.at[:, pl.ds(first, width)], theirs_ref, last_sems.at[1]),
    ]
    for chunk in copies + [last]:
        for copy in chunk:
            copy.start()
    gate = jnp.zeros(hidden_ref.shape, f32)
    up = jnp.zeros(hidden_ref.shape, f32)
    for i, chunk in enumerate(copies):
        for copy in chunk:
            copy.wait()
        block = slice(i * depth, (i + 1) * depth)
        part = held[0][:, block]
        gate += jnp.dot(part, held[1][block], preferred_element_type=f32)
        up += jnp.dot(part, held[2][block], preferred_element_type=f32)
    for copy in last:
        copy.wait()
    hidden = (gate / (1 + jnp.exp(-gate)) * up * mask_ref[...].astype(f32)).astype(bf16)
    hidden_ref[...] = hidden
    columns = width // STEPS
    stores = []
    for i in range(STEPS):
        block = pl.ds(i * columns, columns)
        sent_ref[:, block] = jnp.dot(hidden, theirs_ref[:, block], preferred_element_type=f32).astype(bf16)
        stores.append(pltpu.make_async_copy(sent_ref.at[:, block], away_ref.at[:, block], out_sems.at[i]))
        stores[-1].start()
    for store in stores:
        store.wait()


def sort_body(place_ref, dest_ref, lengths_ref, kv_ref, mark_ref, *out_refs):
    x, mine, first = place_ref[0], place_ref[1], place_ref[2]
    row = lax.broadcasted_iota(jnp.int32, kv_ref.shape[1:], 0) + first
    for r in range(kv_ref.shape[0]):
        d = dest_ref[mine, r]
        value = kv_ref[r]
        value = jnp.where(row < lengths_ref[r], value, jnp.zeros_like(value))
        step = lax.rem(lax.rem(d, SIDE) - x + SIDE, SIDE)
        for k in range(SIDE):

            @pl.when(step == k)
            def _():
                out_refs[k][lax.div(d, SIDE)] = value


def turn_body(place_ref, *refs):
    x, zh = place_ref[0], place_ref[3]
    in_refs, out_refs = refs[:SIDE], refs[SIDE:]
    for k in range(SIDE):
        source = lax.rem(x - k + SIDE, SIDE)
        for out_ref, j in zip(out_refs, ORDER):
            out_ref[source] = in_refs[k][lax.rem(zh + j, SIDE)]


def lay_body(place_ref, *refs):
    zh = place_ref[3]
    in_refs, out_ref = refs[:SIDE], refs[-1]
    for in_ref, j in zip(in_refs, ORDER):
        source = lax.rem(zh - j + SIDE, SIDE)
        for k in range(SIDE):
            out_ref[source * SIDE + k] = in_ref[k]


def add_body(own_ref, arrived_ref, out_ref, mark_ref, total_ref, sems):
    mark_ref[...] = jnp.zeros_like(mark_ref)
    rows = out_ref.shape[0] // STEPS
    copies = []
    for i in range(STEPS):
        block = pl.ds(i * rows, rows)
        total_ref[block] = (own_ref[block] + arrived_ref[block].astype(f32)).astype(bf16)
        copies.append(pltpu.make_async_copy(total_ref.at[block], out_ref.at[block], sems.at[i]))
        copies[-1].start()
    for copy in copies:
        copy.wait()


def sum_body(parts_ref, *refs):
    out_ref, total_ref, sems = refs[-3:]
    total = parts_ref[0].astype(f32)
    for i in range(1, CHIPS):
        total += parts_ref[i].astype(f32)
    total_ref[...] = total.astype(bf16)
    copies = [pltpu.make_async_copy(total_ref, out_ref.at[i], sems.at[i]) for i in range(CHIPS)]
    for copy in copies:
        copy.start()
    for copy in copies:
        copy.wait()


def half_body(which, core_ref, value_ref, *refs):
    out_ref, sems = refs[-2:]
    rows, width = value_ref.shape[0] // STEPS, value_ref.shape[1]
    first = pl.multiple_of((core_ref[0] ^ which) * width, width)
    copies = []
    for i in range(STEPS):
        block = pl.ds(i * rows, rows)
        copies.append(pltpu.make_async_copy(value_ref.at[block], out_ref.at[block, pl.ds(first, width)], sems.at[i]))
        copies[-1].start()
    for copy in copies:
        copy.wait()


def half_of(out_shape, core, value, *into):
    return call(
        lambda *refs: half_body(len(into), *refs),
        out_shape,
        [SMEM, VMEM] + [ANY] * len(into),
        ANY,
        scratch_shapes=[pltpu.SemaphoreType.DMA((STEPS,))],
        input_output_aliases={2: 0} if into else {},
    )(core, value, *into)


def after(value, *others):
    return call(
        lambda *refs: None,
        jax.ShapeDtypeStruct(value.shape, value.dtype),
        [ANY] * (1 + len(others)),
        ANY,
        input_output_aliases={0: 0},
    )(value, *others)


def shift(value, axis, k):
    return lax.ppermute(value, axis, [(i, (i + k) % SIDE) for i in range(SIDE)])


def shards(tokens, gate_weight, up_weight, down_weight, active, kv_blocks, lengths, dest):
    core = lax.axis_index("core")
    x, zh = lax.axis_index("x"), lax.axis_index("zh")
    place = jnp.stack([x, lax.axis_index(GRP), lax.axis_index(TP) * kv_blocks.shape[1], zh])

    rows, width = tokens.shape[0], down_weight.shape[1] // 2
    hidden, away = call(
        hidden_body,
        [jax.ShapeDtypeStruct(active.shape, bf16), pltpu.HBM((rows, width), bf16)],
        [SMEM] + [ANY] * 5,
        [VMEM, ANY],
        vmem=56,
        scratch_shapes=[
            pltpu.VMEM(tokens.shape, bf16),
            pltpu.VMEM(gate_weight.shape, bf16),
            pltpu.VMEM(up_weight.shape, bf16),
            pltpu.VMEM((active.shape[1], width), bf16),
            pltpu.VMEM(active.shape, jnp.int32),
            pltpu.VMEM((rows, width), bf16),
            pltpu.SemaphoreType.DMA((3, CHUNKS)),
            pltpu.SemaphoreType.DMA((2,)),
            pltpu.SemaphoreType.DMA((STEPS,)),
        ],
    )(core[None], tokens, gate_weight, up_weight, down_weight, active)

    ours = lax.dynamic_slice_in_dim(down_weight, core * width, width, 1)
    arrived = lax.ppermute(away, "core", SWAP)
    own = jnp.dot(hidden, ours, preferred_element_type=f32)
    total, mark = call(
        add_body,
        [pltpu.HBM((rows, width), bf16), MARK],
        [VMEM] * 2,
        [ANY, VMEM],
        scratch_shapes=[pltpu.VMEM((rows, width), bf16), pltpu.SemaphoreType.DMA((STEPS,))],
    )(own, arrived)

    parts = total.reshape(CHIPS, rows // CHIPS, width)
    parts = lax.all_to_all(parts, RING, split_axis=0, concat_axis=0, tiled=True)

    slots = jax.ShapeDtypeStruct((SIDE, *kv_blocks.shape[1:]), bf16)
    bundles = call(sort_body, [slots] * SIDE, [SMEM] * 3 + [VMEM] * 2, [VMEM] * SIDE)(
        place, dest, lengths, kv_blocks, mark
    )
    bundles = [bundles[0]] + [shift(bundles[k], "x", k) for k in range(1, SIDE)]
    bundles = call(turn_body, [slots] * SIDE, [SMEM] + [VMEM] * SIDE, [VMEM] * SIDE)(place, *bundles)

    spread = call(
        sum_body,
        pltpu.HBM(parts.shape, bf16),
        [VMEM] + [ANY] * SIDE,
        ANY,
        scratch_shapes=[pltpu.VMEM(parts.shape[1:], bf16), pltpu.SemaphoreType.DMA((CHIPS,))],
    )(parts, *bundles)

    half = lax.all_to_all(spread, RING, split_axis=0, concat_axis=0, tiled=True).reshape(rows, width)

    bundles = [bundles[0]] + [shift(b, "zh", j) for b, j in zip(bundles[1:], ORDER[1:])]
    cache = call(lay_body, jax.ShapeDtypeStruct(kv_blocks.shape, bf16), [SMEM] + [VMEM] * SIDE, VMEM)(place, *bundles)

    half = after(half, *bundles[1:])
    other = lax.ppermute(half, "core", SWAP)
    ffn_out = jax.ShapeDtypeStruct((rows, 2 * width), bf16)
    ffn_out = half_of(ffn_out, core[None], other, half_of(ffn_out, core[None], half))
    return (ffn_out, cache)


def solution(mesh):
    fine = Mesh(mesh.devices.reshape(4, 4, 8, 3, 2), GRP + TP)
    return jax.shard_map(
        shards,
        mesh=fine,
        in_specs=(
            P(GRP, None),
            P(None, TP),
            P(None, TP),
            P(TP, None),
            P(GRP, TP),
            P(GRP, TP, None),
            P(GRP),
            P(),
        ),
        out_specs=(P(GRP, None), P(GRP, TP, None)),
        check_vma=False,
    )
```

```python
import jax
import jax.numpy as jnp
from jax import lax
from jax.experimental import pallas as pl
from jax.experimental.pallas import tpu as pltpu
from jax.sharding import Mesh, PartitionSpec as P

GRP = ("zh", "x")
TP = ("y", "zl", "core")
RING = ("zl", "y")
SWAP = [(0, 1), (1, 0)]
SIDE = 4
CHIPS = 24
ORDER = (0, 2, 1, 3)
CHUNKS = 4
STEPS = 4

bf16, f32 = jnp.bfloat16, jnp.float32
MARK = jax.ShapeDtypeStruct((8, 128), f32)
VMEM = pl.BlockSpec(memory_space=pltpu.VMEM)
SMEM = pl.BlockSpec(memory_space=pltpu.SMEM)
ANY = pl.BlockSpec(memory_space=pl.ANY)


def call(body, out_shape, in_specs, out_specs, vmem=16, **more):
    return pl.pallas_call(
        body,
        out_shape=out_shape,
        in_specs=in_specs,
        out_specs=out_specs,
        cost_estimate=pl.CostEstimate(flops=10**6, bytes_accessed=10**6, transcendentals=0),
        compiler_params=pltpu.CompilerParams(vmem_limit_bytes=vmem * 2**20),
        **more,
    )


def hidden_body(core_ref, tokens_ref, gate_ref, up_ref, down_ref, active_ref, hidden_ref, away_ref, *scratch):
    tokens, weights, theirs_ref, mask_ref, sent_ref, sems, last_sems, out_sems = scratch
    depth, units = tokens_ref.shape[1] // CHUNKS, hidden_ref.shape[1]
    copies = []
    for i in range(CHUNKS):
        block = pl.ds(i * depth, depth)
        copies.append(
            [
                pltpu.make_async_copy(tokens_ref.at[:, block], tokens.at[:, block], sems.at[0, i]),
                pltpu.make_async_copy(gate_ref.at[block], weights.at[block, pl.ds(0, units)], sems.at[1, i]),
                pltpu.make_async_copy(up_ref.at[block], weights.at[block, pl.ds(units, units)], sems.at[2, i]),
            ]
        )
    width = away_ref.shape[1]
    first = pl.multiple_of((1 - core_ref[0]) * width, width)
    last = [
        pltpu.make_async_copy(active_ref, mask_ref, last_sems.at[0]),
        pltpu.make_async_copy(down_ref.at[:, pl.ds(first, width)], theirs_ref, last_sems.at[1]),
    ]
    for chunk in copies + [last]:
        for copy in chunk:
            copy.start()
    both = jnp.zeros((hidden_ref.shape[0], 2 * units), f32)
    for i, chunk in enumerate(copies):
        for copy in chunk:
            copy.wait()
        block = slice(i * depth, (i + 1) * depth)
        both += jnp.dot(tokens[:, block], weights[block], preferred_element_type=f32)
    for copy in last:
        copy.wait()
    gate, up = both[:, :units], both[:, units:]
    hidden = (gate / (1 + jnp.exp(-gate)) * up * mask_ref[...].astype(f32)).astype(bf16)
    hidden_ref[...] = hidden
    columns = width // STEPS
    stores = []
    for i in range(STEPS):
        block = pl.ds(i * columns, columns)
        sent_ref[:, block] = jnp.dot(hidden, theirs_ref[:, block], preferred_element_type=f32).astype(bf16)
        stores.append(pltpu.make_async_copy(sent_ref.at[:, block], away_ref.at[:, block], out_sems.at[i]))
        stores[-1].start()
    for store in stores:
        store.wait()


def sort_body(place_ref, dest_ref, lengths_ref, kv_ref, mark_ref, *out_refs):
    x, mine, first = place_ref[0], place_ref[1], place_ref[2]
    row = lax.broadcasted_iota(jnp.int32, kv_ref.shape[1:], 0) + first
    for r in range(kv_ref.shape[0]):
        d = dest_ref[mine, r]
        value = kv_ref[r]
        value = jnp.where(row < lengths_ref[r], value, jnp.zeros_like(value))
        step = lax.rem(lax.rem(d, SIDE) - x + SIDE, SIDE)
        for k in range(SIDE):

            @pl.when(step == k)
            def _():
                out_refs[k][lax.div(d, SIDE)] = value


def turn_body(place_ref, *refs):
    x, zh = place_ref[0], place_ref[3]
    in_refs, out_refs = refs[:SIDE], refs[SIDE:]
    for k in range(SIDE):
        source = lax.rem(x - k + SIDE, SIDE)
        for out_ref, j in zip(out_refs, ORDER):
            out_ref[source] = in_refs[k][lax.rem(zh + j, SIDE)]


def lay_body(place_ref, *refs):
    zh = place_ref[3]
    in_refs, out_ref = refs[:SIDE], refs[-1]
    for in_ref, j in zip(in_refs, ORDER):
        source = lax.rem(zh - j + SIDE, SIDE)
        for k in range(SIDE):
            out_ref[source * SIDE + k] = in_ref[k]


def add_body(own_ref, arrived_ref, out_ref, mark_ref, total_ref, sems):
    mark_ref[...] = jnp.zeros_like(mark_ref)
    rows = out_ref.shape[0] // STEPS
    copies = []
    for i in range(STEPS):
        block = pl.ds(i * rows, rows)
        total_ref[block] = (own_ref[block] + arrived_ref[block].astype(f32)).astype(bf16)
        copies.append(pltpu.make_async_copy(total_ref.at[block], out_ref.at[block], sems.at[i]))
        copies[-1].start()
    for copy in copies:
        copy.wait()


def sum_body(parts_ref, *refs):
    out_ref, total_ref, sems = refs[-3:]
    total = parts_ref[0].astype(f32)
    for i in range(1, CHIPS):
        total += parts_ref[i].astype(f32)
    total_ref[...] = total.astype(bf16)
    copies = [pltpu.make_async_copy(total_ref, out_ref.at[i], sems.at[i]) for i in range(CHIPS)]
    for copy in copies:
        copy.start()
    for copy in copies:
        copy.wait()


def half_body(which, core_ref, value_ref, *refs):
    out_ref, sems = refs[-2:]
    rows, width = value_ref.shape[0] // STEPS, value_ref.shape[1]
    first = pl.multiple_of((core_ref[0] ^ which) * width, width)
    copies = []
    for i in range(STEPS):
        block = pl.ds(i * rows, rows)
        copies.append(pltpu.make_async_copy(value_ref.at[block], out_ref.at[block, pl.ds(first, width)], sems.at[i]))
        copies[-1].start()
    for copy in copies:
        copy.wait()


def half_of(out_shape, core, value, *into):
    return call(
        lambda *refs: half_body(len(into), *refs),
        out_shape,
        [SMEM, VMEM] + [ANY] * len(into),
        ANY,
        scratch_shapes=[pltpu.SemaphoreType.DMA((STEPS,))],
        input_output_aliases={2: 0} if into else {},
    )(core, value, *into)


def after(value, *others):
    return call(
        lambda *refs: None,
        jax.ShapeDtypeStruct(value.shape, value.dtype),
        [ANY] * (1 + len(others)),
        ANY,
        input_output_aliases={0: 0},
    )(value, *others)


def shift(value, axis, k):
    return lax.ppermute(value, axis, [(i, (i + k) % SIDE) for i in range(SIDE)])


def shards(tokens, gate_weight, up_weight, down_weight, active, kv_blocks, lengths, dest):
    core = lax.axis_index("core")
    x, zh = lax.axis_index("x"), lax.axis_index("zh")
    place = jnp.stack([x, lax.axis_index(GRP), lax.axis_index(TP) * kv_blocks.shape[1], zh])

    rows, width = tokens.shape[0], down_weight.shape[1] // 2
    hidden, away = call(
        hidden_body,
        [jax.ShapeDtypeStruct(active.shape, bf16), pltpu.HBM((rows, width), bf16)],
        [SMEM] + [ANY] * 5,
        [VMEM, ANY],
        vmem=56,
        scratch_shapes=[
            pltpu.VMEM(tokens.shape, bf16),
            pltpu.VMEM((gate_weight.shape[0], 2 * gate_weight.shape[1]), bf16),
            pltpu.VMEM((active.shape[1], width), bf16),
            pltpu.VMEM(active.shape, jnp.int32),
            pltpu.VMEM((rows, width), bf16),
            pltpu.SemaphoreType.DMA((3, CHUNKS)),
            pltpu.SemaphoreType.DMA((2,)),
            pltpu.SemaphoreType.DMA((STEPS,)),
        ],
    )(core[None], tokens, gate_weight, up_weight, down_weight, active)

    ours = lax.dynamic_slice_in_dim(down_weight, core * width, width, 1)
    arrived = lax.ppermute(away, "core", SWAP)
    own = jnp.dot(hidden, ours, preferred_element_type=f32)
    total, mark = call(
        add_body,
        [pltpu.HBM((rows, width), bf16), MARK],
        [VMEM] * 2,
        [ANY, VMEM],
        scratch_shapes=[pltpu.VMEM((rows, width), bf16), pltpu.SemaphoreType.DMA((STEPS,))],
    )(own, arrived)

    parts = total.reshape(CHIPS, rows // CHIPS, width)
    parts = lax.all_to_all(parts, RING, split_axis=0, concat_axis=0, tiled=True)

    slots = jax.ShapeDtypeStruct((SIDE, *kv_blocks.shape[1:]), bf16)
    bundles = call(sort_body, [slots] * SIDE, [SMEM] * 3 + [VMEM] * 2, [VMEM] * SIDE)(
        place, dest, lengths, kv_blocks, mark
    )
    bundles = [bundles[0]] + [shift(bundles[k], "x", k) for k in range(1, SIDE)]
    bundles = call(turn_body, [slots] * SIDE, [SMEM] + [VMEM] * SIDE, [VMEM] * SIDE)(place, *bundles)

    spread = call(
        sum_body,
        pltpu.HBM(parts.shape, bf16),
        [VMEM] + [ANY] * SIDE,
        ANY,
        scratch_shapes=[pltpu.VMEM(parts.shape[1:], bf16), pltpu.SemaphoreType.DMA((CHIPS,))],
    )(parts, *bundles)

    half = lax.all_to_all(spread, RING, split_axis=0, concat_axis=0, tiled=True).reshape(rows, width)

    bundles = [bundles[0]] + [shift(b, "zh", j) for b, j in zip(bundles[1:], ORDER[1:])]
    cache = call(lay_body, jax.ShapeDtypeStruct(kv_blocks.shape, bf16), [SMEM] + [VMEM] * SIDE, VMEM)(place, *bundles)

    half = after(half, *bundles[1:])
    other = lax.ppermute(half, "core", SWAP)
    ffn_out = jax.ShapeDtypeStruct((rows, 2 * width), bf16)
    ffn_out = half_of(ffn_out, core[None], other, half_of(ffn_out, core[None], half))
    return (ffn_out, cache)


def solution(mesh):
    fine = Mesh(mesh.devices.reshape(4, 4, 8, 3, 2), GRP + TP)
    return jax.shard_map(
        shards,
        mesh=fine,
        in_specs=(
            P(GRP, None),
            P(None, TP),
            P(None, TP),
            P(TP, None),
            P(GRP, TP),
            P(GRP, TP, None),
            P(GRP),
            P(),
        ),
        out_specs=(P(GRP, None), P(GRP, TP, None)),
        check_vma=False,
    )
```

```python
import jax
import jax.numpy as jnp
from jax import lax
from jax.experimental import pallas as pl
from jax.experimental.pallas import tpu as pltpu
from jax.sharding import Mesh, PartitionSpec as P

GRP = ("zh", "x")
TP = ("y", "zl", "core")
RING = ("y", "zl")
SWAP = [(0, 1), (1, 0)]
SIDE = 4
CHIPS = 24
ORDER = (0, 2, 1, 3)
CHUNKS = 4
STEPS = 4

bf16, f32 = jnp.bfloat16, jnp.float32
MARK = jax.ShapeDtypeStruct((8, 128), f32)
VMEM = pl.BlockSpec(memory_space=pltpu.VMEM)
SMEM = pl.BlockSpec(memory_space=pltpu.SMEM)
ANY = pl.BlockSpec(memory_space=pl.ANY)


def call(body, out_shape, in_specs, out_specs, vmem=16, **more):
    return pl.pallas_call(
        body,
        out_shape=out_shape,
        in_specs=in_specs,
        out_specs=out_specs,
        cost_estimate=pl.CostEstimate(flops=10**6, bytes_accessed=10**6, transcendentals=0),
        compiler_params=pltpu.CompilerParams(vmem_limit_bytes=vmem * 2**20),
        **more,
    )


def hidden_body(core_ref, tokens_ref, gate_ref, up_ref, down_ref, active_ref, hidden_ref, away_ref, *scratch):
    tokens, weights, theirs_ref, mask_ref, sems, last_sems = scratch
    depth, units = tokens_ref.shape[1] // CHUNKS, hidden_ref.shape[1]
    copies = []
    for i in range(CHUNKS):
        block = pl.ds(i * depth, depth)
        copies.append(
            [
                pltpu.make_async_copy(tokens_ref.at[:, block], tokens.at[:, block], sems.at[0, i]),
                pltpu.make_async_copy(gate_ref.at[block], weights.at[block, pl.ds(0, units)], sems.at[1, i]),
                pltpu.make_async_copy(up_ref.at[block], weights.at[block, pl.ds(units, units)], sems.at[2, i]),
            ]
        )
    width = away_ref.shape[1]
    first = pl.multiple_of((1 - core_ref[0]) * width, width)
    last = [
        pltpu.make_async_copy(active_ref, mask_ref, last_sems.at[0]),
        pltpu.make_async_copy(down_ref.at[:, pl.ds(first, width)], theirs_ref, last_sems.at[1]),
    ]
    for chunk in copies + [last]:
        for copy in chunk:
            copy.start()
    both = jnp.zeros((hidden_ref.shape[0], 2 * units), f32)
    for i, chunk in enumerate(copies):
        for copy in chunk:
            copy.wait()
        block = slice(i * depth, (i + 1) * depth)
        both += jnp.dot(tokens[:, block], weights[block], preferred_element_type=f32)
    for copy in last:
        copy.wait()
    gate, up = both[:, :units], both[:, units:]
    hidden = (gate / (1 + jnp.exp(-gate)) * up * mask_ref[...].astype(f32)).astype(bf16)
    hidden_ref[...] = hidden
    away_ref[...] = jnp.dot(hidden, theirs_ref[...], preferred_element_type=f32).astype(bf16)


def sort_body(place_ref, dest_ref, lengths_ref, kv_ref, mark_ref, *out_refs):
    x, mine, first = place_ref[0], place_ref[1], place_ref[2]
    row = lax.broadcasted_iota(jnp.int32, kv_ref.shape[1:], 0) + first
    for r in range(kv_ref.shape[0]):
        d = dest_ref[mine, r]
        value = kv_ref[r]
        value = jnp.where(row < lengths_ref[r], value, jnp.zeros_like(value))
        step = lax.rem(lax.rem(d, SIDE) - x + SIDE, SIDE)
        for k in range(SIDE):

            @pl.when(step == k)
            def _():
                out_refs[k][lax.div(d, SIDE)] = value


def turn_body(place_ref, *refs):
    x, zh = place_ref[0], place_ref[3]
    in_refs, out_refs = refs[:SIDE], refs[SIDE:]
    for k in range(SIDE):
        source = lax.rem(x - k + SIDE, SIDE)
        for out_ref, j in zip(out_refs, ORDER):
            out_ref[source] = in_refs[k][lax.rem(zh + j, SIDE)]


def lay_body(place_ref, *refs):
    zh = place_ref[3]
    in_refs, out_ref = refs[:SIDE], refs[-1]
    for in_ref, j in zip(in_refs, ORDER):
        source = lax.rem(zh - j + SIDE, SIDE)
        for k in range(SIDE):
            out_ref[source * SIDE + k] = in_ref[k]


def add_body(own_ref, arrived_ref, out_ref, mark_ref, total_ref, sems):
    mark_ref[...] = jnp.zeros_like(mark_ref)
    rows = out_ref.shape[0] // STEPS
    copies = []
    for i in range(STEPS):
        block = pl.ds(i * rows, rows)
        total_ref[block] = (own_ref[block] + arrived_ref[block].astype(f32)).astype(bf16)
        copies.append(pltpu.make_async_copy(total_ref.at[block], out_ref.at[block], sems.at[i]))
        copies[-1].start()
    for copy in copies:
        copy.wait()


def sum_body(parts_ref, *refs):
    out_ref, total_ref, sems = refs[-3:]
    total = parts_ref[0].astype(f32)
    for i in range(1, CHIPS):
        total += parts_ref[i].astype(f32)
    total_ref[...] = total.astype(bf16)
    copies = [pltpu.make_async_copy(total_ref, out_ref.at[i], sems.at[i]) for i in range(CHIPS)]
    for copy in copies:
        copy.start()
    for copy in copies:
        copy.wait()


def half_body(which, core_ref, value_ref, *refs):
    out_ref, sems = refs[-2:]
    rows, width = value_ref.shape[0] // STEPS, value_ref.shape[1]
    first = pl.multiple_of((core_ref[0] ^ which) * width, width)
    copies = []
    for i in range(STEPS):
        block = pl.ds(i * rows, rows)
        copies.append(pltpu.make_async_copy(value_ref.at[block], out_ref.at[block, pl.ds(first, width)], sems.at[i]))
        copies[-1].start()
    for copy in copies:
        copy.wait()


def half_of(out_shape, core, value, *into):
    return call(
        lambda *refs: half_body(len(into), *refs),
        out_shape,
        [SMEM, VMEM] + [ANY] * len(into),
        ANY,
        scratch_shapes=[pltpu.SemaphoreType.DMA((STEPS,))],
        input_output_aliases={2: 0} if into else {},
    )(core, value, *into)


def after(value, *others):
    return call(
        lambda *refs: None,
        jax.ShapeDtypeStruct(value.shape, value.dtype),
        [ANY] * (1 + len(others)),
        ANY,
        input_output_aliases={0: 0},
    )(value, *others)


def shift(value, axis, k):
    return lax.ppermute(value, axis, [(i, (i + k) % SIDE) for i in range(SIDE)])


def shards(tokens, gate_weight, up_weight, down_weight, active, kv_blocks, lengths, dest):
    core = lax.axis_index("core")
    x, zh = lax.axis_index("x"), lax.axis_index("zh")
    place = jnp.stack([x, lax.axis_index(GRP), lax.axis_index(TP) * kv_blocks.shape[1], zh])

    rows, width = tokens.shape[0], down_weight.shape[1] // 2
    hidden, away = call(
        hidden_body,
        [pltpu.VMEM(active.shape, bf16), pltpu.VMEM((rows, width), bf16)],
        [SMEM] + [ANY] * 5,
        [VMEM, VMEM],
        vmem=56,
        scratch_shapes=[
            pltpu.VMEM(tokens.shape, bf16),
            pltpu.VMEM((gate_weight.shape[0], 2 * gate_weight.shape[1]), bf16),
            pltpu.VMEM((active.shape[1], width), bf16),
            pltpu.VMEM(active.shape, jnp.int32),
            pltpu.SemaphoreType.DMA((3, CHUNKS)),
            pltpu.SemaphoreType.DMA((2,)),
        ],
    )(core[None], tokens, gate_weight, up_weight, down_weight, active)

    ours = lax.dynamic_slice_in_dim(down_weight, core * width, width, 1)
    arrived = lax.ppermute(away, "core", SWAP)
    own = jnp.dot(hidden, ours, preferred_element_type=f32)
    total, mark = call(
        add_body,
        [pltpu.HBM((rows, width), bf16), MARK],
        [VMEM] * 2,
        [ANY, VMEM],
        scratch_shapes=[pltpu.VMEM((rows, width), bf16), pltpu.SemaphoreType.DMA((STEPS,))],
    )(own, arrived)

    parts = total.reshape(CHIPS, rows // CHIPS, width)
    parts = lax.all_to_all(parts, RING, split_axis=0, concat_axis=0, tiled=True)

    slots = jax.ShapeDtypeStruct((SIDE, *kv_blocks.shape[1:]), bf16)
    bundles = call(sort_body, [slots] * SIDE, [SMEM] * 3 + [VMEM] * 2, [VMEM] * SIDE)(
        place, dest, lengths, kv_blocks, mark
    )
    bundles = [bundles[0]] + [shift(bundles[k], "x", k) for k in range(1, SIDE)]
    bundles = call(turn_body, [slots] * SIDE, [SMEM] + [VMEM] * SIDE, [VMEM] * SIDE)(place, *bundles)

    spread = call(
        sum_body,
        pltpu.HBM(parts.shape, bf16),
        [VMEM] + [ANY] * SIDE,
        ANY,
        scratch_shapes=[pltpu.VMEM(parts.shape[1:], bf16), pltpu.SemaphoreType.DMA((CHIPS,))],
    )(parts, *bundles)

    half = lax.all_to_all(spread, RING, split_axis=0, concat_axis=0, tiled=True).reshape(rows, width)

    bundles = [bundles[0]] + [shift(b, "zh", j) for b, j in zip(bundles[1:], ORDER[1:])]
    cache = call(lay_body, jax.ShapeDtypeStruct(kv_blocks.shape, bf16), [SMEM] + [VMEM] * SIDE, VMEM)(place, *bundles)

    half = after(half, *bundles[1:])
    other = lax.ppermute(half, "core", SWAP)
    ffn_out = jax.ShapeDtypeStruct((rows, 2 * width), bf16)
    ffn_out = half_of(ffn_out, core[None], other, half_of(ffn_out, core[None], half))
    return (ffn_out, cache)


def solution(mesh):
    fine = Mesh(mesh.devices.reshape(4, 4, 8, 3, 2), GRP + TP)
    return jax.shard_map(
        shards,
        mesh=fine,
        in_specs=(
            P(GRP, None),
            P(None, TP),
            P(None, TP),
            P(TP, None),
            P(GRP, TP),
            P(GRP, TP, None),
            P(GRP),
            P(),
        ),
        out_specs=(P(GRP, None), P(GRP, TP, None)),
        check_vma=False,
    )
```

```python
import jax
import jax.numpy as jnp
from jax import lax
from jax.experimental import pallas as pl
from jax.experimental.pallas import tpu as pltpu
from jax.sharding import Mesh, PartitionSpec as P

GRP = ("zh", "x")
TP = ("y", "zl", "core")
RING = ("y", "zl")
SWAP = [(0, 1), (1, 0)]
SIDE = 4
CHIPS = 24
ORDER = (0, 2, 1, 3)
CHUNKS = 4
STEPS = 4

bf16, f32 = jnp.bfloat16, jnp.float32
MARK = jax.ShapeDtypeStruct((8, 128), f32)
VMEM = pl.BlockSpec(memory_space=pltpu.VMEM)
SMEM = pl.BlockSpec(memory_space=pltpu.SMEM)
ANY = pl.BlockSpec(memory_space=pl.ANY)


def call(body, out_shape, in_specs, out_specs, vmem=16, **more):
    return pl.pallas_call(
        body,
        out_shape=out_shape,
        in_specs=in_specs,
        out_specs=out_specs,
        cost_estimate=pl.CostEstimate(flops=10**6, bytes_accessed=10**6, transcendentals=0),
        compiler_params=pltpu.CompilerParams(vmem_limit_bytes=vmem * 2**20),
        **more,
    )


def hidden_body(core_ref, tokens_ref, gate_ref, up_ref, down_ref, active_ref, hidden_ref, away_ref, *scratch):
    tokens, weights, theirs_ref, mask_ref, sems, last_sems = scratch
    depth, units = tokens_ref.shape[1] // CHUNKS, hidden_ref.shape[1]
    copies = []
    for i in range(CHUNKS):
        block = pl.ds(i * depth, depth)
        copies.append(
            [
                pltpu.make_async_copy(tokens_ref.at[:, block], tokens.at[:, block], sems.at[0, i]),
                pltpu.make_async_copy(gate_ref.at[block], weights.at[block, pl.ds(0, units)], sems.at[1, i]),
                pltpu.make_async_copy(up_ref.at[block], weights.at[block, pl.ds(units, units)], sems.at[2, i]),
            ]
        )
    width = away_ref.shape[1]
    first = pl.multiple_of((1 - core_ref[0]) * width, width)
    last = [
        pltpu.make_async_copy(active_ref, mask_ref, last_sems.at[0]),
        pltpu.make_async_copy(down_ref.at[:, pl.ds(first, width)], theirs_ref, last_sems.at[1]),
    ]
    for chunk in copies + [last]:
        for copy in chunk:
            copy.start()
    both = jnp.zeros((hidden_ref.shape[0], 2 * units), f32)
    for i, chunk in enumerate(copies):
        for copy in chunk:
            copy.wait()
        block = slice(i * depth, (i + 1) * depth)
        both += jnp.dot(tokens[:, block], weights[block], preferred_element_type=f32)
    for copy in last:
        copy.wait()
    gate, up = both[:, :units], both[:, units:]
    hidden = (gate / (1 + jnp.exp(-gate)) * up * mask_ref[...].astype(f32)).astype(bf16)
    hidden_ref[...] = hidden
    away_ref[...] = jnp.dot(hidden, theirs_ref[...], preferred_element_type=f32).astype(bf16)


def sort_body(place_ref, dest_ref, lengths_ref, kv_ref, mark_ref, *out_refs):
    mine, first, zh = place_ref[1], place_ref[2], place_ref[3]
    row = lax.broadcasted_iota(jnp.int32, kv_ref.shape[1:], 0) + first
    for r in range(kv_ref.shape[0]):
        d = dest_ref[mine, r]
        value = kv_ref[r]
        value = jnp.where(row < lengths_ref[r], value, jnp.zeros_like(value))
        step = lax.rem(lax.div(d, SIDE) - zh + SIDE, SIDE)
        for out_ref, j in zip(out_refs, ORDER):

            @pl.when(step == j)
            def _():
                out_ref[lax.rem(d, SIDE)] = value


def turn_body(place_ref, *refs):
    x, zh = place_ref[0], place_ref[3]
    in_refs, out_refs = refs[:SIDE], refs[SIDE:]
    for in_ref, j in zip(in_refs, ORDER):
        source = lax.rem(zh - j + SIDE, SIDE)
        for k, out_ref in enumerate(out_refs):
            out_ref[source] = in_ref[lax.rem(x + k, SIDE)]


def lay_body(place_ref, *refs):
    x = place_ref[0]
    in_refs, out_ref = refs[:SIDE], refs[-1]
    for k, in_ref in enumerate(in_refs):
        column = lax.rem(x - k + SIDE, SIDE)
        for source in range(SIDE):
            out_ref[source * SIDE + column] = in_ref[source]


def add_body(own_ref, arrived_ref, out_ref, mark_ref, total_ref, sems):
    mark_ref[...] = jnp.zeros_like(mark_ref)
    rows = out_ref.shape[0] // STEPS
    copies = []
    for i in range(STEPS):
        block = pl.ds(i * rows, rows)
        total_ref[block] = (own_ref[block] + arrived_ref[block].astype(f32)).astype(bf16)
        copies.append(pltpu.make_async_copy(total_ref.at[block], out_ref.at[block], sems.at[i]))
        copies[-1].start()
    for copy in copies:
        copy.wait()


def sum_body(parts_ref, *refs):
    out_ref, total_ref, sems = refs[-3:]
    total = parts_ref[0].astype(f32)
    for i in range(1, CHIPS):
        total += parts_ref[i].astype(f32)
    total_ref[...] = total.astype(bf16)
    copies = [pltpu.make_async_copy(total_ref, out_ref.at[i], sems.at[i]) for i in range(CHIPS)]
    for copy in copies:
        copy.start()
    for copy in copies:
        copy.wait()


def half_body(which, core_ref, value_ref, *refs):
    out_ref, sems = refs[-2:]
    rows, width = value_ref.shape[0] // STEPS, value_ref.shape[1]
    first = pl.multiple_of((core_ref[0] ^ which) * width, width)
    copies = []
    for i in range(STEPS):
        block = pl.ds(i * rows, rows)
        copies.append(pltpu.make_async_copy(value_ref.at[block], out_ref.at[block, pl.ds(first, width)], sems.at[i]))
        copies[-1].start()
    for copy in copies:
        copy.wait()


def half_of(out_shape, core, value, *into):
    return call(
        lambda *refs: half_body(len(into), *refs),
        out_shape,
        [SMEM, VMEM] + [ANY] * len(into),
        ANY,
        scratch_shapes=[pltpu.SemaphoreType.DMA((STEPS,))],
        input_output_aliases={2: 0} if into else {},
    )(core, value, *into)


def after(value, *others):
    return call(
        lambda *refs: None,
        jax.ShapeDtypeStruct(value.shape, value.dtype),
        [ANY] * (1 + len(others)),
        ANY,
        input_output_aliases={0: 0},
    )(value, *others)


def shift(value, axis, k):
    return lax.ppermute(value, axis, [(i, (i + k) % SIDE) for i in range(SIDE)])


def shards(tokens, gate_weight, up_weight, down_weight, active, kv_blocks, lengths, dest):
    core = lax.axis_index("core")
    x, zh = lax.axis_index("x"), lax.axis_index("zh")
    place = jnp.stack([x, lax.axis_index(GRP), lax.axis_index(TP) * kv_blocks.shape[1], zh])

    rows, width = tokens.shape[0], down_weight.shape[1] // 2
    hidden, away = call(
        hidden_body,
        [pltpu.VMEM(active.shape, bf16), pltpu.VMEM((rows, width), bf16)],
        [SMEM] + [ANY] * 5,
        [VMEM, VMEM],
        vmem=56,
        scratch_shapes=[
            pltpu.VMEM(tokens.shape, bf16),
            pltpu.VMEM((gate_weight.shape[0], 2 * gate_weight.shape[1]), bf16),
            pltpu.VMEM((active.shape[1], width), bf16),
            pltpu.VMEM(active.shape, jnp.int32),
            pltpu.SemaphoreType.DMA((3, CHUNKS)),
            pltpu.SemaphoreType.DMA((2,)),
        ],
    )(core[None], tokens, gate_weight, up_weight, down_weight, active)

    ours = lax.dynamic_slice_in_dim(down_weight, core * width, width, 1)
    arrived = lax.ppermute(away, "core", SWAP)
    own = jnp.dot(hidden, ours, preferred_element_type=f32)
    total, mark = call(
        add_body,
        [pltpu.HBM((rows, width), bf16), MARK],
        [VMEM] * 2,
        [ANY, VMEM],
        scratch_shapes=[pltpu.VMEM((rows, width), bf16), pltpu.SemaphoreType.DMA((STEPS,))],
    )(own, arrived)

    parts = total.reshape(CHIPS, rows // CHIPS, width)
    parts = lax.all_to_all(parts, RING, split_axis=0, concat_axis=0, tiled=True)

    slots = jax.ShapeDtypeStruct((SIDE, *kv_blocks.shape[1:]), bf16)
    bundles = call(sort_body, [slots] * SIDE, [SMEM] * 3 + [VMEM] * 2, [VMEM] * SIDE)(
        place, dest, lengths, kv_blocks, mark
    )
    bundles = [bundles[0]] + [shift(b, "zh", j) for b, j in zip(bundles[1:], ORDER[1:])]
    bundles = call(turn_body, [slots] * SIDE, [SMEM] + [VMEM] * SIDE, [VMEM] * SIDE)(place, *bundles)

    spread = call(
        sum_body,
        pltpu.HBM(parts.shape, bf16),
        [VMEM] + [ANY] * SIDE,
        ANY,
        scratch_shapes=[pltpu.VMEM(parts.shape[1:], bf16), pltpu.SemaphoreType.DMA((CHIPS,))],
    )(parts, *bundles)

    half = lax.all_to_all(spread, RING, split_axis=0, concat_axis=0, tiled=True).reshape(rows, width)

    bundles = [bundles[0]] + [shift(bundles[k], "x", k) for k in range(1, SIDE)]
    cache = call(lay_body, jax.ShapeDtypeStruct(kv_blocks.shape, bf16), [SMEM] + [VMEM] * SIDE, VMEM)(place, *bundles)

    half = after(half, *bundles[1:])
    other = lax.ppermute(half, "core", SWAP)
    ffn_out = jax.ShapeDtypeStruct((rows, 2 * width), bf16)
    ffn_out = half_of(ffn_out, core[None], other, half_of(ffn_out, core[None], half))
    return (ffn_out, cache)


def solution(mesh):
    fine = Mesh(mesh.devices.reshape(4, 4, 8, 3, 2), GRP + TP)
    return jax.shard_map(
        shards,
        mesh=fine,
        in_specs=(
            P(GRP, None),
            P(None, TP),
            P(None, TP),
            P(TP, None),
            P(GRP, TP),
            P(GRP, TP, None),
            P(GRP),
            P(),
        ),
        out_specs=(P(GRP, None), P(GRP, TP, None)),
        check_vma=False,
    )
```

```python
import jax
import jax.numpy as jnp
from jax import lax
from jax.experimental import pallas as pl
from jax.experimental.pallas import tpu as pltpu
from jax.sharding import Mesh, PartitionSpec as P

GRP = ("zh", "x")
TP = ("y", "zl", "core")
RING = ("y", "zl")
SWAP = [(0, 1), (1, 0)]
SIDE = 4
CHIPS = 24
ORDER = (0, 2, 1, 3)
CHUNKS = 4
STEPS = 4

bf16, f32 = jnp.bfloat16, jnp.float32
MARK = jax.ShapeDtypeStruct((8, 128), f32)
VMEM = pl.BlockSpec(memory_space=pltpu.VMEM)
SMEM = pl.BlockSpec(memory_space=pltpu.SMEM)
ANY = pl.BlockSpec(memory_space=pl.ANY)


def call(body, out_shape, in_specs, out_specs, vmem=16, **more):
    return pl.pallas_call(
        body,
        out_shape=out_shape,
        in_specs=in_specs,
        out_specs=out_specs,
        cost_estimate=pl.CostEstimate(flops=10**6, bytes_accessed=10**6, transcendentals=0),
        compiler_params=pltpu.CompilerParams(vmem_limit_bytes=vmem * 2**20),
        **more,
    )


def hidden_body(core_ref, tokens_ref, gate_ref, up_ref, down_ref, active_ref, hidden_ref, away_ref, *scratch):
    tokens, weights, theirs_ref, mask_ref, sems, last_sems = scratch
    depth, units = tokens_ref.shape[1] // CHUNKS, hidden_ref.shape[1]
    copies = []
    for i in range(CHUNKS):
        block = pl.ds(i * depth, depth)
        copies.append(
            [
                pltpu.make_async_copy(tokens_ref.at[:, block], tokens.at[:, block], sems.at[0, i]),
                pltpu.make_async_copy(gate_ref.at[block], weights.at[block, pl.ds(0, units)], sems.at[1, i]),
                pltpu.make_async_copy(up_ref.at[block], weights.at[block, pl.ds(units, units)], sems.at[2, i]),
            ]
        )
    width = away_ref.shape[1]
    first = pl.multiple_of((1 - core_ref[0]) * width, width)
    last = [
        pltpu.make_async_copy(active_ref, mask_ref, last_sems.at[0]),
        pltpu.make_async_copy(down_ref.at[:, pl.ds(first, width)], theirs_ref, last_sems.at[1]),
    ]
    for chunk in copies + [last]:
        for copy in chunk:
            copy.start()
    both = jnp.zeros((hidden_ref.shape[0], 2 * units), f32)
    for i, chunk in enumerate(copies):
        for copy in chunk:
            copy.wait()
        block = slice(i * depth, (i + 1) * depth)
        both += jnp.dot(tokens[:, block], weights[block], preferred_element_type=f32)
    for copy in last:
        copy.wait()
    gate, up = both[:, :units], both[:, units:]
    hidden = (gate / (1 + jnp.exp(-gate)) * up * mask_ref[...].astype(f32)).astype(bf16)
    hidden_ref[...] = hidden
    away_ref[...] = jnp.dot(hidden, theirs_ref[...], preferred_element_type=f32).astype(bf16)


def own_body(core_ref, hidden_ref, down_ref, out_ref, ours_ref, sems):
    width = out_ref.shape[1]
    columns = width // STEPS
    first = core_ref[0] * width
    copies = []
    for i in range(STEPS):
        source = pl.ds(pl.multiple_of(first + i * columns, columns), columns)
        copies.append(
            pltpu.make_async_copy(down_ref.at[:, source], ours_ref.at[:, pl.ds(i * columns, columns)], sems.at[i])
        )
        copies[-1].start()
    for i, copy in enumerate(copies):
        copy.wait()
        block = slice(i * columns, (i + 1) * columns)
        out_ref[:, block] = jnp.dot(hidden_ref[...], ours_ref[:, block], preferred_element_type=f32)


def sort_body(place_ref, dest_ref, lengths_ref, kv_ref, mark_ref, *out_refs):
    x, mine, first = place_ref[0], place_ref[1], place_ref[2]
    row = lax.broadcasted_iota(jnp.int32, kv_ref.shape[1:], 0) + first
    for r in range(kv_ref.shape[0]):
        d = dest_ref[mine, r]
        value = kv_ref[r]
        value = jnp.where(row < lengths_ref[r], value, jnp.zeros_like(value))
        step = lax.rem(lax.rem(d, SIDE) - x + SIDE, SIDE)
        for k in range(SIDE):

            @pl.when(step == k)
            def _():
                out_refs[k][lax.div(d, SIDE)] = value


def turn_body(place_ref, *refs):
    x, zh = place_ref[0], place_ref[3]
    in_refs, out_refs = refs[:SIDE], refs[SIDE:]
    for k in range(SIDE):
        source = lax.rem(x - k + SIDE, SIDE)
        for out_ref, j in zip(out_refs, ORDER):
            out_ref[source] = in_refs[k][lax.rem(zh + j, SIDE)]


def lay_body(place_ref, *refs):
    zh = place_ref[3]
    in_refs, out_ref = refs[:SIDE], refs[-1]
    for in_ref, j in zip(in_refs, ORDER):
        source = lax.rem(zh - j + SIDE, SIDE)
        for k in range(SIDE):
            out_ref[source * SIDE + k] = in_ref[k]


def add_body(own_ref, arrived_ref, out_ref, mark_ref, total_ref, sems):
    mark_ref[...] = jnp.zeros_like(mark_ref)
    rows = out_ref.shape[0] // STEPS
    copies = []
    for i in range(STEPS):
        block = pl.ds(i * rows, rows)
        total_ref[block] = (own_ref[block] + arrived_ref[block].astype(f32)).astype(bf16)
        copies.append(pltpu.make_async_copy(total_ref.at[block], out_ref.at[block], sems.at[i]))
        copies[-1].start()
    for copy in copies:
        copy.wait()


def sum_body(parts_ref, *refs):
    out_ref, total_ref, sems = refs[-3:]
    total = parts_ref[0].astype(f32)
    for i in range(1, CHIPS):
        total += parts_ref[i].astype(f32)
    total_ref[...] = total.astype(bf16)
    copies = [pltpu.make_async_copy(total_ref, out_ref.at[i], sems.at[i]) for i in range(CHIPS)]
    for copy in copies:
        copy.start()
    for copy in copies:
        copy.wait()


def half_body(which, core_ref, value_ref, *refs):
    out_ref, sems = refs[-2:]
    rows, width = value_ref.shape[0] // STEPS, value_ref.shape[1]
    first = pl.multiple_of((core_ref[0] ^ which) * width, width)
    copies = []
    for i in range(STEPS):
        block = pl.ds(i * rows, rows)
        copies.append(pltpu.make_async_copy(value_ref.at[block], out_ref.at[block, pl.ds(first, width)], sems.at[i]))
        copies[-1].start()
    for copy in copies:
        copy.wait()


def half_of(out_shape, core, value, *into):
    return call(
        lambda *refs: half_body(len(into), *refs),
        out_shape,
        [SMEM, VMEM] + [ANY] * len(into),
        ANY,
        scratch_shapes=[pltpu.SemaphoreType.DMA((STEPS,))],
        input_output_aliases={2: 0} if into else {},
    )(core, value, *into)


def after(value, *others):
    return call(
        lambda *refs: None,
        jax.ShapeDtypeStruct(value.shape, value.dtype),
        [ANY] * (1 + len(others)),
        ANY,
        input_output_aliases={0: 0},
    )(value, *others)


def shift(value, axis, k):
    return lax.ppermute(value, axis, [(i, (i + k) % SIDE) for i in range(SIDE)])


def shards(tokens, gate_weight, up_weight, down_weight, active, kv_blocks, lengths, dest):
    core = lax.axis_index("core")
    x, zh = lax.axis_index("x"), lax.axis_index("zh")
    place = jnp.stack([x, lax.axis_index(GRP), lax.axis_index(TP) * kv_blocks.shape[1], zh])

    rows, width = tokens.shape[0], down_weight.shape[1] // 2
    hidden, away = call(
        hidden_body,
        [pltpu.VMEM(active.shape, bf16), pltpu.VMEM((rows, width), bf16)],
        [SMEM] + [ANY] * 5,
        [VMEM, VMEM],
        vmem=56,
        scratch_shapes=[
            pltpu.VMEM(tokens.shape, bf16),
            pltpu.VMEM((gate_weight.shape[0], 2 * gate_weight.shape[1]), bf16),
            pltpu.VMEM((active.shape[1], width), bf16),
            pltpu.VMEM(active.shape, jnp.int32),
            pltpu.SemaphoreType.DMA((3, CHUNKS)),
            pltpu.SemaphoreType.DMA((2,)),
        ],
    )(core[None], tokens, gate_weight, up_weight, down_weight, active)

    arrived = lax.ppermute(away, "core", SWAP)
    own = call(
        own_body,
        pltpu.VMEM((rows, width), f32),
        [SMEM, VMEM, ANY],
        VMEM,
        vmem=50,
        scratch_shapes=[pltpu.VMEM((down_weight.shape[0], width), bf16), pltpu.SemaphoreType.DMA((STEPS,))],
    )(core[None], hidden, down_weight)
    total, mark = call(
        add_body,
        [pltpu.HBM((rows, width), bf16), MARK],
        [VMEM] * 2,
        [ANY, VMEM],
        scratch_shapes=[pltpu.VMEM((rows, width), bf16), pltpu.SemaphoreType.DMA((STEPS,))],
    )(own, arrived)

    parts = total.reshape(CHIPS, rows // CHIPS, width)
    parts = lax.all_to_all(parts, RING, split_axis=0, concat_axis=0, tiled=True)

    slots = jax.ShapeDtypeStruct((SIDE, *kv_blocks.shape[1:]), bf16)
    bundles = call(sort_body, [slots] * SIDE, [SMEM] * 3 + [VMEM] * 2, [VMEM] * SIDE)(
        place, dest, lengths, kv_blocks, mark
    )
    bundles = [bundles[0]] + [shift(bundles[k], "x", k) for k in range(1, SIDE)]
    bundles = call(turn_body, [slots] * SIDE, [SMEM] + [VMEM] * SIDE, [VMEM] * SIDE)(place, *bundles)

    spread = call(
        sum_body,
        pltpu.HBM(parts.shape, bf16),
        [VMEM] + [ANY] * SIDE,
        ANY,
        scratch_shapes=[pltpu.VMEM(parts.shape[1:], bf16), pltpu.SemaphoreType.DMA((CHIPS,))],
    )(parts, *bundles)

    half = lax.all_to_all(spread, RING, split_axis=0, concat_axis=0, tiled=True).reshape(rows, width)

    bundles = [bundles[0]] + [shift(b, "zh", j) for b, j in zip(bundles[1:], ORDER[1:])]
    cache = call(lay_body, jax.ShapeDtypeStruct(kv_blocks.shape, bf16), [SMEM] + [VMEM] * SIDE, VMEM)(place, *bundles)

    half = after(half, *bundles[1:])
    other = lax.ppermute(half, "core", SWAP)
    ffn_out = jax.ShapeDtypeStruct((rows, 2 * width), bf16)
    ffn_out = half_of(ffn_out, core[None], other, half_of(ffn_out, core[None], half))
    return (ffn_out, cache)


def solution(mesh):
    fine = Mesh(mesh.devices.reshape(4, 4, 8, 3, 2), GRP + TP)
    return jax.shard_map(
        shards,
        mesh=fine,
        in_specs=(
            P(GRP, None),
            P(None, TP),
            P(None, TP),
            P(TP, None),
            P(GRP, TP),
            P(GRP, TP, None),
            P(GRP),
            P(),
        ),
        out_specs=(P(GRP, None), P(GRP, TP, None)),
        check_vma=False,
    )
```

```python
import jax
import jax.numpy as jnp
from jax import lax
from jax.experimental import pallas as pl
from jax.experimental.pallas import tpu as pltpu
from jax.sharding import Mesh, PartitionSpec as P

GRP = ("zh", "x")
TP = ("y", "zl", "core")
RING = ("y", "zl")
SWAP = [(0, 1), (1, 0)]
SIDE = 4
CHIPS = 24
ORDER = (0, 2, 3, 1)
CHUNKS = 4
STEPS = 4

bf16, f32 = jnp.bfloat16, jnp.float32
MARK = jax.ShapeDtypeStruct((8, 128), f32)
VMEM = pl.BlockSpec(memory_space=pltpu.VMEM)
SMEM = pl.BlockSpec(memory_space=pltpu.SMEM)
ANY = pl.BlockSpec(memory_space=pl.ANY)


def call(body, out_shape, in_specs, out_specs, vmem=16, **more):
    return pl.pallas_call(
        body,
        out_shape=out_shape,
        in_specs=in_specs,
        out_specs=out_specs,
        cost_estimate=pl.CostEstimate(flops=10**6, bytes_accessed=10**6, transcendentals=0),
        compiler_params=pltpu.CompilerParams(vmem_limit_bytes=vmem * 2**20),
        **more,
    )


def hidden_body(core_ref, tokens_ref, gate_ref, up_ref, down_ref, active_ref, hidden_ref, away_ref, *scratch):
    tokens, weights, theirs_ref, mask_ref, sems, last_sems = scratch
    depth, units = tokens_ref.shape[1] // CHUNKS, hidden_ref.shape[1]
    copies = []
    for i in range(CHUNKS):
        block = pl.ds(i * depth, depth)
        copies.append(
            [
                pltpu.make_async_copy(tokens_ref.at[:, block], tokens.at[:, block], sems.at[0, i]),
                pltpu.make_async_copy(gate_ref.at[block], weights.at[block, pl.ds(0, units)], sems.at[1, i]),
                pltpu.make_async_copy(up_ref.at[block], weights.at[block, pl.ds(units, units)], sems.at[2, i]),
            ]
        )
    width = away_ref.shape[1]
    first = pl.multiple_of((1 - core_ref[0]) * width, width)
    last = [
        pltpu.make_async_copy(active_ref, mask_ref, last_sems.at[0]),
        pltpu.make_async_copy(down_ref.at[:, pl.ds(first, width)], theirs_ref, last_sems.at[1]),
    ]
    for chunk in copies + [last]:
        for copy in chunk:
            copy.start()
    both = jnp.zeros((hidden_ref.shape[0], 2 * units), f32)
    for i, chunk in enumerate(copies):
        for copy in chunk:
            copy.wait()
        block = slice(i * depth, (i + 1) * depth)
        both += jnp.dot(tokens[:, block], weights[block], preferred_element_type=f32)
    for copy in last:
        copy.wait()
    gate, up = both[:, :units], both[:, units:]
    hidden = (gate / (1 + jnp.exp(-gate)) * up * mask_ref[...].astype(f32)).astype(bf16)
    hidden_ref[...] = hidden
    away_ref[...] = jnp.dot(hidden, theirs_ref[...], preferred_element_type=f32).astype(bf16)


def own_body(core_ref, hidden_ref, down_ref, out_ref, ours_ref, sems):
    width = out_ref.shape[1]
    columns = width // STEPS
    first = core_ref[0] * width
    copies = []
    for i in range(STEPS):
        source = pl.ds(pl.multiple_of(first + i * columns, columns), columns)
        copies.append(
            pltpu.make_async_copy(down_ref.at[:, source], ours_ref.at[:, pl.ds(i * columns, columns)], sems.at[i])
        )
        copies[-1].start()
    for i, copy in enumerate(copies):
        copy.wait()
        block = slice(i * columns, (i + 1) * columns)
        out_ref[:, block] = jnp.dot(hidden_ref[...], ours_ref[:, block], preferred_element_type=f32)


def sort_body(place_ref, dest_ref, lengths_ref, kv_ref, mark_ref, *out_refs):
    x, mine, first = place_ref[0], place_ref[1], place_ref[2]
    row = lax.broadcasted_iota(jnp.int32, kv_ref.shape[1:], 0) + first
    for r in range(kv_ref.shape[0]):
        d = dest_ref[mine, r]
        value = kv_ref[r]
        value = jnp.where(row < lengths_ref[r], value, jnp.zeros_like(value))
        step = lax.rem(lax.rem(d, SIDE) - x + SIDE, SIDE)
        for k in range(SIDE):

            @pl.when(step == k)
            def _():
                out_refs[k][lax.div(d, SIDE)] = value


def turn_body(place_ref, *refs):
    x, zh = place_ref[0], place_ref[3]
    in_refs, out_refs = refs[:SIDE], refs[SIDE:]
    for k in range(SIDE):
        source = lax.rem(x - k + SIDE, SIDE)
        for out_ref, j in zip(out_refs, ORDER):
            out_ref[source] = in_refs[k][lax.rem(zh + j, SIDE)]


def lay_body(place_ref, *refs):
    zh = place_ref[3]
    in_refs, out_ref = refs[:SIDE], refs[-1]
    for in_ref, j in zip(in_refs, ORDER):
        source = lax.rem(zh - j + SIDE, SIDE)
        for k in range(SIDE):
            out_ref[source * SIDE + k] = in_ref[k]


def add_body(own_ref, arrived_ref, out_ref, mark_ref, total_ref, sems):
    mark_ref[...] = jnp.zeros_like(mark_ref)
    rows = out_ref.shape[0] // STEPS
    copies = []
    for i in range(STEPS):
        block = pl.ds(i * rows, rows)
        total_ref[block] = (own_ref[block] + arrived_ref[block].astype(f32)).astype(bf16)
        copies.append(pltpu.make_async_copy(total_ref.at[block], out_ref.at[block], sems.at[i]))
        copies[-1].start()
    for copy in copies:
        copy.wait()


def sum_body(parts_ref, *refs):
    out_ref, total_ref, sems = refs[-3:]
    total = parts_ref[0].astype(f32)
    for i in range(1, CHIPS):
        total += parts_ref[i].astype(f32)
    total_ref[...] = total.astype(bf16)
    copies = [pltpu.make_async_copy(total_ref, out_ref.at[i], sems.at[i]) for i in range(CHIPS)]
    for copy in copies:
        copy.start()
    for copy in copies:
        copy.wait()


def half_body(which, core_ref, value_ref, *refs):
    out_ref, sems = refs[-2:]
    rows, width = value_ref.shape[0] // STEPS, value_ref.shape[1]
    first = pl.multiple_of((core_ref[0] ^ which) * width, width)
    copies = []
    for i in range(STEPS):
        block = pl.ds(i * rows, rows)
        copies.append(pltpu.make_async_copy(value_ref.at[block], out_ref.at[block, pl.ds(first, width)], sems.at[i]))
        copies[-1].start()
    for copy in copies:
        copy.wait()


def half_of(out_shape, core, value, *into):
    return call(
        lambda *refs: half_body(len(into), *refs),
        out_shape,
        [SMEM, VMEM] + [ANY] * len(into),
        ANY,
        scratch_shapes=[pltpu.SemaphoreType.DMA((STEPS,))],
        input_output_aliases={2: 0} if into else {},
    )(core, value, *into)


def after(value, *others):
    return call(
        lambda *refs: None,
        jax.ShapeDtypeStruct(value.shape, value.dtype),
        [ANY] * (1 + len(others)),
        ANY,
        input_output_aliases={0: 0},
    )(value, *others)


def shift(value, axis, k):
    return lax.ppermute(value, axis, [(i, (i + k) % SIDE) for i in range(SIDE)])


def shards(tokens, gate_weight, up_weight, down_weight, active, kv_blocks, lengths, dest):
    core = lax.axis_index("core")
    x, zh = lax.axis_index("x"), lax.axis_index("zh")
    place = jnp.stack([x, lax.axis_index(GRP), lax.axis_index(TP) * kv_blocks.shape[1], zh])

    rows, width = tokens.shape[0], down_weight.shape[1] // 2
    hidden, away = call(
        hidden_body,
        [pltpu.VMEM(active.shape, bf16), pltpu.VMEM((rows, width), bf16)],
        [SMEM] + [ANY] * 5,
        [VMEM, VMEM],
        vmem=56,
        scratch_shapes=[
            pltpu.VMEM(tokens.shape, bf16),
            pltpu.VMEM((gate_weight.shape[0], 2 * gate_weight.shape[1]), bf16),
            pltpu.VMEM((active.shape[1], width), bf16),
            pltpu.VMEM(active.shape, jnp.int32),
            pltpu.SemaphoreType.DMA((3, CHUNKS)),
            pltpu.SemaphoreType.DMA((2,)),
        ],
    )(core[None], tokens, gate_weight, up_weight, down_weight, active)

    arrived = lax.ppermute(away, "core", SWAP)
    own = call(
        own_body,
        pltpu.VMEM((rows, width), f32),
        [SMEM, VMEM, ANY],
        VMEM,
        vmem=50,
        scratch_shapes=[pltpu.VMEM((down_weight.shape[0], width), bf16), pltpu.SemaphoreType.DMA((STEPS,))],
    )(core[None], hidden, down_weight)
    total, mark = call(
        add_body,
        [pltpu.HBM((rows, width), bf16), MARK],
        [VMEM] * 2,
        [ANY, VMEM],
        scratch_shapes=[pltpu.VMEM((rows, width), bf16), pltpu.SemaphoreType.DMA((STEPS,))],
    )(own, arrived)

    parts = total.reshape(CHIPS, rows // CHIPS, width)
    parts = lax.all_to_all(parts, RING, split_axis=0, concat_axis=0, tiled=True)

    slots = jax.ShapeDtypeStruct((SIDE, *kv_blocks.shape[1:]), bf16)
    bundles = call(sort_body, [slots] * SIDE, [SMEM] * 3 + [VMEM] * 2, [VMEM] * SIDE)(
        place, dest, lengths, kv_blocks, mark
    )
    bundles = [bundles[0]] + [shift(bundles[k], "x", k) for k in range(1, SIDE)]
    bundles = call(turn_body, [slots] * SIDE, [SMEM] + [VMEM] * SIDE, [VMEM] * SIDE)(place, *bundles)

    spread = call(
        sum_body,
        pltpu.HBM(parts.shape, bf16),
        [VMEM] + [ANY] * SIDE,
        ANY,
        scratch_shapes=[pltpu.VMEM(parts.shape[1:], bf16), pltpu.SemaphoreType.DMA((CHIPS,))],
    )(parts, *bundles)

    half = lax.all_to_all(spread, RING, split_axis=0, concat_axis=0, tiled=True).reshape(rows, width)

    bundles = [bundles[0]] + [shift(b, "zh", j) for b, j in zip(bundles[1:], ORDER[1:])]
    cache = call(lay_body, jax.ShapeDtypeStruct(kv_blocks.shape, bf16), [SMEM] + [VMEM] * SIDE, VMEM)(place, *bundles)

    half = after(half, *bundles[1:])
    other = lax.ppermute(half, "core", SWAP)
    ffn_out = jax.ShapeDtypeStruct((rows, 2 * width), bf16)
    ffn_out = half_of(ffn_out, core[None], other, half_of(ffn_out, core[None], half))
    return (ffn_out, cache)


def solution(mesh):
    fine = Mesh(mesh.devices.reshape(4, 4, 8, 3, 2), GRP + TP)
    return jax.shard_map(
        shards,
        mesh=fine,
        in_specs=(
            P(GRP, None),
            P(None, TP),
            P(None, TP),
            P(TP, None),
            P(GRP, TP),
            P(GRP, TP, None),
            P(GRP),
            P(),
        ),
        out_specs=(P(GRP, None), P(GRP, TP, None)),
        check_vma=False,
    )
```
